512 devices in a mesh: chain: 64 (over z, y), rows: 8 (over x, core).
Axes of the slice: x: 4, y: 4, z: 16, core: 2. Of those that a mesh axis runs over, the one named last changes fastest.
Arguments:
- sites: float32 [64, 512, 2, 512], P('chain', 'rows'), as said below
- angles: float32 [64, 2], P('chain'), may hold values from -3.140625 to 3.140625
- sketch: float32 [1024, 512], replicated, may hold values from -0.1875 to 0.1875
Outputs:
- new_sites: float32 [64, 512, 2, 512], P('chain', 'rows')
The draws below stay inside these ranges and needn't reach their ends.
Inputs may be any that keep to these rules, and one draw needn't show every extreme that they name: `sites`: real site tensors.
All inputs are finite; a program needn't handle non-finite values.
Results may differ from the reference program's by a relative error of at most 0.0003.
Values sent between devices are 32-bit elements; how exact they have to be, the bound alone decides.
A program may use at most 64 MiB of HBM per device.

```python
import math
import jax
import jax.numpy as jnp
from jax import lax

CHI = 512
ITERS = 6
SITES = 64


def draw_sites(key, part):
    key = jax.random.fold_in(key, 3)
    first, second, third = jax.random.split(key, 3)
    shape = (SITES, CHI, 2, CHI)
    core = jax.random.normal(first, shape, jnp.float32)
    lower, upper = (0.3, 3.0)
    row_scale = jnp.exp(jax.random.uniform(second, (SITES, CHI, 1, 1), jnp.float32, math.log(lower), math.log(upper)))
    col_scale = jnp.exp(jax.random.uniform(third, (SITES, 1, 1, CHI), jnp.float32, math.log(lower), math.log(upper)))
    return core * row_scale * col_scale / math.sqrt(CHI)


def noise(key, extent, deviation, bound, held_as=jnp.bfloat16):
    entries = jax.random.normal(key, extent, jnp.float32) * deviation
    return jnp.minimum(jnp.maximum(entries, -bound), bound).astype(held_as)


def setup_inputs(seed: int = 0) -> dict:
    seeds = jax.random.split(jax.random.key(seed), 4)
    return {
        "sites": draw_sites(jax.random.fold_in(seeds[3], 71), 0),
        "angles": jnp.clip(jax.random.uniform(seeds[1], (SITES, 2), jnp.float32, -3.140625, 3.140625), -3.140625, 3.140625),
        "sketch": noise(seeds[2], (2 * CHI, CHI), (2 * CHI) ** -0.5, 0.1875, jnp.float32),
    }


HIGH = lax.Precision.HIGHEST

def rotation(angle):
    cosine = jnp.cos(angle)
    sine = jnp.sin(angle)
    return jnp.stack([jnp.stack([cosine, -sine]), jnp.stack([sine, cosine])])

def gate_of(left_angles, right_angles):
    coupling = 0.5 * (left_angles[1] + right_angles[1])
    kick = jnp.kron(rotation(left_angles[0]), rotation(right_angles[0]))
    flip = jnp.kron(jnp.array([[0.0, 1.0], [-1.0, 0.0]], jnp.float32), jnp.array([[0.0, 1.0], [1.0, 0.0]], jnp.float32))
    mixer = jnp.cos(coupling) * jnp.eye(4, dtype=jnp.float32) + jnp.sin(coupling) * flip
    return jnp.dot(kick, mixer, precision=HIGH)

def bond(pair_sites, pair_angles, sketch):
    left = pair_sites[0].reshape(2 * CHI, CHI)
    right = pair_sites[1].reshape(CHI, 2 * CHI)
    theta = jnp.dot(left, right, precision=HIGH).reshape(CHI, 2, 2, CHI)
    gate = gate_of(pair_angles[0], pair_angles[1]).reshape(2, 2, 2, 2)
    theta = jnp.einsum('pqst,lstr->lpqr', gate, theta, precision=HIGH).reshape(2 * CHI, 2 * CHI)
    sketched = jnp.dot(theta, sketch, precision=HIGH)
    gram = jnp.dot(sketched.T, sketched, precision=HIGH)
    scale = jnp.sqrt(jnp.sum(gram * gram) + 1e-06)
    normed = gram / scale
    inverse = jnp.eye(CHI, dtype=jnp.float32)
    for step in range(ITERS):
        product = jnp.dot(jnp.dot(jnp.dot(inverse, normed, precision=HIGH), inverse, precision=HIGH), inverse, precision=HIGH)
        inverse = 1.5 * inverse - 0.5 * product
    basis = jnp.dot(sketched, inverse, precision=HIGH) * jnp.sqrt(2.0 * CHI / scale)
    new_right = jnp.dot(basis.T, theta, precision=HIGH) / (2.0 * CHI)
    return jnp.stack([basis.reshape(CHI, 2, CHI), new_right.reshape(CHI, 2, CHI)])

def reference(sites, angles, sketch):
    paired = sites.reshape(SITES // 2, 2, CHI, 2, CHI)
    paired_angles = angles.reshape(SITES // 2, 2, 2)
    result = lax.map(lambda item: bond(item[0], item[1], sketch), (paired, paired_angles))
    return result.reshape(SITES, CHI, 2, CHI)
```

```python
import functools

import jax
import jax.numpy as jnp
from jax import lax
from jax.experimental import pallas as pl
from jax.experimental.pallas import tpu as pltpu
from jax.sharding import PartitionSpec as P

ITERS = 6
MESH = pl.DeviceIdType.MESH
F32 = jnp.float32
BF16 = jnp.bfloat16

GA, GS, GL = 0, 1, 2
PRI, SEC, FWD, B0, B1, B2, B3 = range(7)


def split(x):
    high = x.astype(BF16)
    return high, (x - high.astype(F32)).astype(BF16)


def dot3(a, b, contract=((1,), (0,))):
    ah, al = a
    bh, bl = b
    d = functools.partial(
        lax.dot_general, dimension_numbers=(contract, ((), ())), preferred_element_type=F32
    )
    return d(ah, bh) + (d(ah, bl) + d(al, bh))


def kernel(
    sites, angles, sketch, out,
    buf, lbuf, sbuf, wbuf, wh, wl, zf, zh, zl, ah, al, xbuf, obuf, ang,
    ss, rs, vs, vr, bs, br, loc,
):
    chain = lax.axis_index("chain")
    row = lax.axis_index("rows")
    parity = lax.rem(chain, 2)
    core = lax.rem(row, 2)
    place = lax.div(row, 2)
    half = sites.shape[1]
    width = sites.shape[3]
    turn = 1 - 2 * core
    xs = lax.axis_size("rows") // 2

    def at(step):
        return lax.rem(place + step + xs, xs)

    ahead, behind, across = at(turn), at(-turn), at(2)
    dev_ahead = (chain, 2 * ahead + core)
    dev_behind = (chain, 2 * behind + core)
    dev_sib = (chain, 2 * place + 1 - core)
    dev_y = (chain + 1 - 2 * parity, row)
    blk_own, blk_behind, blk_ahead, blk_across = (
        row, 2 * behind + core, 2 * ahead + core, 2 * across + core,
    )
    sib_own, sib_behind, sib_ahead, sib_across = (
        2 * place + 1 - core, 2 * behind + 1 - core, 2 * ahead + 1 - core, 2 * across + 1 - core,
    )

    def rows(block):
        return pl.ds(pl.multiple_of(half * block, half), half)

    barrier = pltpu.get_barrier_semaphore()
    for device in (dev_ahead, dev_behind, dev_sib, dev_y):
        pl.semaphore_signal(barrier, inc=1, device_id=device, device_id_type=MESH)

    def remote(src, dst, send, recv, device):
        return pltpu.make_async_remote_copy(
            src_ref=src, dst_ref=dst, send_sem=send, recv_sem=recv,
            device_id=device, device_id_type=MESH,
        )

    def piece(which, kind, c, view, block, device):
        ref = view.at[c, rows(block)]
        return remote(ref, ref, ss.at[which, kind, c], rs.at[which, kind, c], device)

    sends = {
        PRI: (blk_own, dev_ahead), SEC: (blk_own, dev_behind), FWD: (blk_behind, dev_ahead),
        B0: (blk_own, dev_sib), B1: (blk_behind, dev_sib),
        B2: (blk_ahead, dev_sib), B3: (blk_across, dev_sib),
    }
    gets = {
        PRI: blk_behind, SEC: blk_ahead, FWD: blk_across,
        B0: sib_own, B1: sib_ahead, B2: sib_behind, B3: sib_across,
    }

    def send(which, kind, view, chunks=(0, 1)):
        for c in chunks:
            piece(which, kind, c, view, *sends[kind]).start()

    def get(which, kind, view, chunks=(0, 1)):
        for c in chunks:
            piece(which, kind, c, view, gets[kind], dev_sib).wait_recv()

    def drain(which, kinds, view):
        for kind in kinds:
            for c in range(2):
                piece(which, kind, c, view, *sends[kind]).wait_send()

    raw, proj = buf.at[0], buf.at[1]
    ring = buf.at[1 - parity]

    def own_copy(view, s):
        return pltpu.make_async_copy(sites.at[0, :, s], view.at[s, rows(blk_own)], loc.at[s])

    def rsib(c, block):
        ref = raw.at[c, rows(block)]
        return ref

    def load_sites(view):
        for s in range(2):
            own_copy(view, s).start()
        for s in range(2):
            own_copy(view, s).wait()

    for n in range(2):
        ang[parity, 8 * n : 8 * n + 8, :] = jnp.full((8, 128), angles[0, n], F32)

    def project(block):
        kick = ang[1, 0:8, :]
        cb, sb = jnp.cos(kick)[0:1, 0:1], jnp.sin(kick)[0:1, 0:1]
        r0, r1 = raw[0, rows(block), :], raw[1, rows(block), :]
        p, q = cb * r0 - sb * r1, sb * r0 + cb * r1
        u, v = cb * r1 - sb * r0, cb * r0 + sb * r1
        lhs = jnp.concatenate(
            [jnp.concatenate([p, q], 1), jnp.concatenate([u, v], 1)], 0
        )
        result = dot3(split(lhs), (wh[...], wl[...]))
        proj[0, rows(block), :] = result[:half]
        proj[1, rows(block), :] = result[half:]

    @pl.when(parity == 0)
    def _():
        load_sites(lbuf)

    @pl.when(parity == 1)
    def _():
        fetch = pltpu.make_async_copy(sketch, wbuf, loc.at[2])
        fetch.start()
        load_sites(raw)
        fetch.wait()
        high, low = split(wbuf[...])
        wh[...] = high
        wl[...] = low
        project(blk_own)

    pl.semaphore_wait(barrier, 4)

    def ang_copy(site):
        return remote(ang.at[site], ang.at[site], vs.at[4], vr.at[4], dev_y)

    def over_y(c, view):
        ref = view.at[c, rows(blk_own)]
        return remote(ref, ref, vs.at[c], vr.at[c], dev_y)

    @pl.when(parity == 1)
    def _():
        send(GA, PRI, ring)
        for c in range(2):
            over_y(c, proj).start()
        send(GA, SEC, ring)
        send(GA, B0, proj)
        ang_copy(parity).start()

    @pl.when(parity == 0)
    def _():
        ang_copy(parity).start()
        for c in range(2):
            over_y(c, lbuf).start()
        for c in range(2):
            over_y(c, proj).wait_recv()
            send(GA, PRI, ring, (c,))
            send(GA, SEC, ring, (c,))
            send(GA, B0, proj, (c,))

    def arrived(kind, then, block, passed):
        for c in range(2):
            get(GA, kind, ring, (c,))
            for other, view in then:
                send(GA, other, view, (c,))

        @pl.when(parity == 1)
        def _():
            project(block)

        send(GA, passed, proj)

    arrived(PRI, [(FWD, ring)], blk_behind, B1)
    arrived(SEC, [], blk_ahead, B2)
    arrived(FWD, [], blk_across, B3)

    ang_copy(1 - parity).wait_recv()

    @pl.when(parity == 1)
    def _():
        for c in range(2):
            over_y(c, lbuf).wait_recv()

    kick, turn_l, turn_r = ang[0, 0:8, :], ang[0, 8:16, :], ang[1, 8:16, :]
    coupling = 0.5 * (turn_l + turn_r)
    ca, sa = jnp.cos(kick)[0:1, 0:1], jnp.sin(kick)[0:1, 0:1]
    cj, sj = jnp.cos(coupling)[0:1, 0:1], jnp.sin(coupling)[0:1, 0:1]
    l0, l1 = lbuf[0, rows(blk_own), :], lbuf[1, rows(blk_own), :]
    p, q = ca * l0 - sa * l1, sa * l0 + ca * l1
    lhs = jnp.concatenate(
        [jnp.concatenate([cj * p, sj * q], 1), jnp.concatenate([cj * q, -sj * p], 1)], 0
    )
    for kind in (B0, B1, B2, B3):
        get(GA, kind, proj)
    own = dot3(split(lhs), split(proj[...].reshape(2 * width, width)))
    sbuf[0, rows(blk_own), :] = own[:half]
    sbuf[1, rows(blk_own), :] = own[half:]

    for c in range(2):
        send(GS, PRI, sbuf, (c,))
    for c in range(2):
        send(GS, SEC, sbuf, (c,))
    send(GS, B0, sbuf)
    for kind, then in ((PRI, (FWD, B1)), (SEC, (B2,)), (FWD, (B3,))):
        for c in range(2):
            get(GS, kind, sbuf, (c,))
            for other in then:
                send(GS, other, sbuf, (c,))
    def sibling_r(n, c, block):
        ref = raw.at[c, rows(block)]
        return remote(ref, ref, bs.at[n, c], br.at[n, c], dev_sib)

    own_blocks = (blk_own, blk_behind, blk_ahead, blk_across)
    sib_blocks = (sib_own, sib_ahead, sib_behind, sib_across)

    @pl.when(parity == 1)
    def _():
        send(GL, PRI, lbuf)
        send(GL, SEC, lbuf)
        send(GL, B0, lbuf)

    for kind in (B0, B1, B2, B3):
        get(GS, kind, sbuf)

    stacked = split(sbuf[...].reshape(2 * width, width))
    gram = dot3(stacked, stacked, ((0,), (0,)))
    scale = jnp.sqrt(jnp.sum(gram * gram, keepdims=True).reshape(1, 1) + 1e-06)
    zf[...] = gram / scale
    at_row = lax.broadcasted_iota(jnp.int32, (2 * half, width), 0)
    at_col = lax.broadcasted_iota(jnp.int32, (2 * half, width), 1)
    unit = jnp.where((at_col == at_row + half * row) & (at_row < half), 1.0, 0.0).astype(F32)
    xbuf[...] = jnp.where(parity == 0, own, unit)

    def refine(step, carry):
        z = zf[...]
        x = xbuf[...]
        z2 = split(z)
        x2 = split(x)
        lhs2 = tuple(jnp.concatenate([a, b], 0) for a, b in zip(z2, x2))
        both = dot3(lhs2, z2)
        square, moved = both[:width], both[width:]
        xbuf[...] = 1.5 * x - 0.5 * moved
        cube = dot3(split(square), z2)
        zf[...] = 2.25 * z - 1.5 * square + 0.25 * cube

        @pl.when((parity == 1) & (step == 0))
        def _():
            for n, block in enumerate(own_blocks):
                for c in range(2):
                    sibling_r(n, c, block).start()

        @pl.when((parity == 1) & (step == 2))
        def _():
            get(GL, PRI, lbuf)
            send(GL, FWD, lbuf)
            send(GL, B1, lbuf)

        @pl.when((parity == 1) & (step == 3))
        def _():
            get(GL, SEC, lbuf)
            send(GL, B2, lbuf)

        @pl.when((parity == 1) & (step == ITERS - 2))
        def _():
            get(GL, FWD, lbuf)
            send(GL, B3, lbuf)

        return carry

    lax.fori_loop(0, ITERS - 1, refine, 0)
    x = xbuf[...]
    x = 1.5 * x - 0.5 * dot3(split(x), split(zf[...]))

    gain = jnp.sqrt(2.0 * width / scale)

    @pl.when(parity == 0)
    def _():
        obuf[...] = (x * gain).reshape(2, half, width)

    @pl.when(parity == 1)
    def _():
        for kind in (B0, B1, B2, B3):
            get(GL, kind, lbuf)
        for n, block in enumerate(sib_blocks):
            for c in range(2):
                sibling_r(n, c, block).wait_recv()
        cols = split(x[:half] * gain)
        e0 = dot3(cols, split(sbuf[0]), ((1,), (1,)))
        e1 = dot3(cols, split(sbuf[1]), ((1,), (1,)))
        f, g = ca * e0 + sa * e1, ca * e1 - sa * e0
        lhs = jnp.concatenate(
            [jnp.concatenate([cj * f, cj * g], 1), jnp.concatenate([-sj * g, sj * f], 1)], 0
        )
        core_mat = dot3(split(lhs), split(lbuf[...].reshape(2 * width, width)))
        c0, c1 = core_mat[:half], core_mat[half:]
        kick_r = ang[1, 0:8, :]
        cb, sb = jnp.cos(kick_r)[0:1, 0:1], jnp.sin(kick_r)[0:1, 0:1]
        k00, k01 = cb * c0 - sb * c1, cb * c1 - sb * c0
        k10, k11 = sb * c0 + cb * c1, cb * c0 + sb * c1
        lhs = jnp.concatenate(
            [jnp.concatenate([k00, k01], 1), jnp.concatenate([k10, k11], 1)], 0
        )
        right = dot3(split(lhs), split(raw[...].reshape(2 * width, width)))
        obuf[...] = (right * (1.0 / (2.0 * width))).reshape(2, half, width)

    stores = [
        pltpu.make_async_copy(obuf.at[s], out.at[0, :, s], loc.at[s]) for s in range(2)
    ]
    for store in stores:
        store.start()

    ang_copy(parity).wait_send()

    @pl.when(parity == 0)
    def _():
        for c in range(2):
            over_y(c, lbuf).wait_send()

    @pl.when(parity == 1)
    def _():
        for c in range(2):
            over_y(c, proj).wait_send()
        drain(GL, range(7), lbuf)
        for n, block in enumerate(own_blocks):
            for c in range(2):
                sibling_r(n, c, block).wait_send()

    drain(GA, (PRI, SEC, FWD), ring)
    drain(GA, (B0, B1, B2, B3), proj)
    drain(GS, range(7), sbuf)
    for store in stores:
        store.wait()


def per_device(sites, angles, sketch):
    half, width = sites.shape[1], sites.shape[3]
    dma = pltpu.SemaphoreType.DMA
    return pl.pallas_call(
        kernel,
        out_shape=jax.ShapeDtypeStruct(sites.shape, F32),
        in_specs=[
            pl.BlockSpec(memory_space=pl.ANY),
            pl.BlockSpec(memory_space=pltpu.SMEM),
            pl.BlockSpec(memory_space=pl.ANY),
        ],
        out_specs=pl.BlockSpec(memory_space=pl.ANY),
        scratch_shapes=[
            pltpu.VMEM((2, 2, width, width), F32),
            pltpu.VMEM((2, width, width), F32),
            pltpu.VMEM((2, width, width), F32),
            pltpu.VMEM((2 * width, width), F32),
            pltpu.VMEM((2 * width, width), BF16),
            pltpu.VMEM((2 * width, width), BF16),
            pltpu.VMEM((width, width), F32),
            pltpu.VMEM((width, width), BF16),
            pltpu.VMEM((width, width), BF16),
            pltpu.VMEM((width + 2 * half, width), BF16),
            pltpu.VMEM((width + 2 * half, width), BF16),
            pltpu.VMEM((2 * half, width), F32),
            pltpu.VMEM((2, half, width), F32),
            pltpu.VMEM((2, 16, 128), F32),
            dma((3, 7, 2)), dma((3, 7, 2)),
            dma((5,)), dma((5,)),
            dma((4, 2)), dma((4, 2)),
            dma((3,)),
        ],
        compiler_params=pltpu.CompilerParams(
            collective_id=0, has_side_effects=True, vmem_limit_bytes=56 * 2**20
        ),
        cost_estimate=pl.CostEstimate(
            flops=20 * 6 * width**3, bytes_accessed=3 * 2**20, transcendentals=0
        ),
    )(sites, angles, sketch)


def solution(mesh):
    in_specs = (P("chain", "rows", None, None), P("chain", None), P())
    out_specs = P("chain", "rows", None, None)
    return jax.shard_map(
        per_device, mesh=mesh, in_specs=in_specs, out_specs=out_specs, check_vma=False
    )
```

```python
import functools

import jax
import jax.numpy as jnp
from jax import lax
from jax.experimental import pallas as pl
from jax.experimental.pallas import tpu as pltpu
from jax.sharding import PartitionSpec as P

ITERS = 6
MESH = pl.DeviceIdType.MESH
F32 = jnp.float32
BF16 = jnp.bfloat16
CUT = 128

RP, RM, FW, B0, BM, BP, BX = range(7)
G_RWA, G_RWB, G_SA, G_SB, G_R, G_L = range(6)
Y_RW, Y_SB, Y_ANG, Y_L = range(4)


def split(x):
    high = x.astype(BF16)
    return high, (x - high.astype(F32)).astype(BF16)


def dot3(a, b, contract=((1,), (0,))):
    ah, al = a
    bh, bl = b
    d = functools.partial(
        lax.dot_general, dimension_numbers=(contract, ((), ())), preferred_element_type=F32
    )
    return d(ah, bh) + (d(ah, bl) + d(al, bh))


def beside(*parts):
    return jnp.concatenate(parts, 1)


def above(*parts):
    return jnp.concatenate(parts, 0)


def kernel(
    sites, angles, sketch, out,
    raw, lbuf, rwa, rwb, sa_, sb_, wbuf, wh, wl, zf, xbuf, obuf, ang, trig,
    ss, rs, vs, vr, loc,
):
    chain = lax.axis_index("chain")
    row = lax.axis_index("rows")
    parity = lax.rem(chain, 2)
    core = lax.rem(row, 2)
    place = lax.div(row, 2)
    half, width = sites.shape[1], sites.shape[3]
    xs = lax.axis_size("rows") // 2
    is_left, is_right = parity == 0, parity == 1

    def at(step):
        return lax.rem(place + step + xs, xs)

    plus, minus, across = at(1), at(-1), at(2)
    dev_plus = (chain, 2 * plus + core)
    dev_minus = (chain, 2 * minus + core)
    dev_sib = (chain, 2 * place + 1 - core)
    dev_y = (chain + 1 - 2 * parity, row)

    barrier = pltpu.get_barrier_semaphore()
    for device in (dev_plus, dev_minus, dev_sib, dev_y):
        pl.semaphore_signal(barrier, inc=1, device_id=device, device_id_type=MESH)

    def rows(block):
        return pl.ds(pl.multiple_of(half * block, half), half)

    own = rows(row)

    def chunk(view, block, c, count):
        part = 2 * half // count
        start = half * block + part * (c % (count // 2))
        return view.at[c // (count // 2), pl.ds(pl.multiple_of(start, part), part)]

    def remote(ref, send, recv, device):
        return pltpu.make_async_remote_copy(
            src_ref=ref, dst_ref=ref, send_sem=send, recv_sem=recv,
            device_id=device, device_id_type=MESH,
        )

    blk_minus, blk_plus, blk_across = (2 * n + core for n in (minus, plus, across))
    sib_own, sib_minus, sib_plus, sib_across = (
        2 * n + 1 - core for n in (place, minus, plus, across)
    )
    sends = {
        RP: (row, dev_plus), RM: (row, dev_minus), B0: (row, dev_sib),
        BM: (blk_minus, dev_sib), BP: (blk_plus, dev_sib), BX: (blk_across, dev_sib),
    }
    gets = {
        RP: blk_minus, RM: blk_plus, FW: blk_across,
        B0: sib_own, BM: sib_minus, BP: sib_plus, BX: sib_across,
    }

    class Ring:
        def __init__(self, view, which, count, shared=True):
            self.view, self.which, self.count, self.shared = view, which, count, shared
            self.low, self.high = range(count // 2), range(count // 2, count)

        def copy(self, kind, c, block, device):
            ref = chunk(self.view, block, c, self.count)
            return remote(ref, ss.at[self.which, kind, c], rs.at[self.which, kind, c], device)

        def sent(self, kind, c):
            if kind == FW:
                passed = (blk_minus, dev_plus) if c in self.low else (blk_plus, dev_minus)
                return self.copy(FW, c, *passed)
            return self.copy(kind, c, *sends[kind])

        def send(self, kind, c):
            self.sent(kind, c).start()

        def get(self, kind, c):
            self.copy(kind, c, gets[kind], dev_sib).wait_recv()

        def issue(self):
            for c, d in zip(self.low, self.high):
                self.send(RP, c)
                self.send(RM, d)
            for c, d in zip(self.low, self.high):
                self.send(RP, d)
                self.send(RM, c)
            self.share(B0)

        def share(self, kind):
            if self.shared:
                for c in range(self.count):
                    self.send(kind, c)

        def issue_chunk(self, c):
            for kind in (RP, RM, B0):
                self.send(kind, c)

        def step1(self):
            for c, d in zip(self.low, self.high):
                self.get(RP, c)
                self.send(FW, c)
                self.get(RM, d)
                self.send(FW, d)
                if self.shared:
                    self.send(BM, c)
                    self.send(BP, d)

        def step2(self):
            for c, d in zip(self.low, self.high):
                self.get(RP, d)
                self.get(RM, c)
                if self.shared:
                    self.send(BM, d)
                    self.send(BP, c)

        def step3(self):
            for c, d in zip(self.low, self.high):
                for n in (c, d):
                    self.get(FW, n)
                    if self.shared:
                        self.send(BX, n)

        def finish(self, *kinds):
            for kind in kinds:
                for c in range(self.count):
                    self.get(kind, c)

        def drain(self, kinds=range(7)):
            for kind in kinds:
                for c in range(self.count):
                    self.sent(kind, c).wait_send()

    ring_rwa, ring_rwb = Ring(rwa, G_RWA, 2), Ring(rwb, G_RWB, 4)
    ring_sa, ring_sb = Ring(sa_, G_SA, 2), Ring(sb_, G_SB, 4)
    ring_r, ring_l = Ring(raw, G_R, 4), Ring(lbuf, G_L, 4, shared=False)
    chip_l = Ring(lbuf, G_L, 4)

    def over_y(view, which, c, count, block=row):
        return remote(chunk(view, block, c, count), vs.at[which, c], vr.at[which, c], dev_y)

    l_blocks = (row, blk_minus, blk_plus, blk_across)

    def l_over_y(n, c):
        return over_y(lbuf, Y_L + n, c, 4, l_blocks[n])

    def ang_copy(site):
        return remote(ang.at[site], vs.at[Y_ANG, 0], vr.at[Y_ANG, 0], dev_y)

    def load_sites(view):
        copies = [
            pltpu.make_async_copy(sites.at[0, :, s], view.at[s, own], loc.at[s]) for s in range(2)
        ]
        for copy in copies:
            copy.start()
        for copy in copies:
            copy.wait()

    for n in range(2):
        ang[parity, 8 * n : 8 * n + 8, :] = jnp.full((8, 128), angles[0, n], F32)

    def scalar(n):
        return trig[n, 0:1, 0:1]

    @pl.when(is_left)
    def _():
        load_sites(lbuf)

    @pl.when(is_right)
    def _():
        fetch = pltpu.make_async_copy(sketch, wbuf, loc.at[2])
        fetch.start()
        load_sites(raw)
        kick = ang[1, 0:8, :]
        trig[4] = jnp.cos(kick)
        trig[5] = jnp.sin(kick)
        cb, sb = scalar(4), scalar(5)
        r0, r1 = raw[0, own, :], raw[1, own, :]
        mixed = above(
            beside(cb * r0 - sb * r1, sb * r0 + cb * r1),
            beside(cb * r1 - sb * r0, cb * r0 + sb * r1),
        )
        fetch.wait()
        high, low = split(wbuf[...])
        wh[...] = high
        wl[...] = low
        result = dot3(split(mixed), (wh[...], wl[...]))
        for m in range(2):
            rwa[m, own, :] = result[half * m : half * (m + 1), :CUT]
            rwb[m, own, :] = result[half * m : half * (m + 1), CUT:]

    pl.semaphore_wait(barrier, 4)

    def all_trig():
        ang_copy(1 - parity).wait_recv()
        kick, coupling = ang[0, 0:8, :], 0.5 * (ang[0, 8:16, :] + ang[1, 8:16, :])
        trig[0] = jnp.cos(kick)
        trig[1] = jnp.sin(kick)
        trig[2] = jnp.cos(coupling)
        trig[3] = jnp.sin(coupling)

    def rows_of_s(view, into):
        ca, sa, cj, sj = (scalar(n) for n in range(4))
        l0, l1 = lbuf[0, own, :], lbuf[1, own, :]
        p, q = ca * l0 - sa * l1, sa * l0 + ca * l1
        lhs = above(beside(cj * p, sj * q), beside(cj * q, -sj * p))
        result = dot3(split(lhs), split(view[...].reshape(2 * width, view.shape[2])))
        for s in range(2):
            into[s, own, :] = result[half * s : half * (s + 1)]

    @pl.when(is_right)
    def _():
        ang_copy(parity).start()
        for c in range(2):
            over_y(rwa, Y_RW, c, 2).start()
        ring_rwb.issue()
        ring_rwb.step1()
        ring_rwa.issue()
        ring_rwb.step2()
        all_trig()
        for c in range(4):
            l_over_y(0, c).wait_recv()
        ring_rwa.step1()
        ring_rwb.step3()
        ring_rwb.finish(B0, BM, BP, BX)
        rows_of_s(rwb, sb_)
        for c in (0, 2, 1, 3):
            over_y(sb_, Y_SB, c, 4).start()
        ring_sb.issue()
        ring_rwa.step2()
        ring_rwa.step3()
        ring_rwa.finish(B0, BM, BP, BX)
        rows_of_s(rwa, sa_)
        ring_sa.issue()
        chip_l.share(B0)
        ring_sb.step1()
        ring_sa.step1()
        ring_sb.step2()
        ring_sa.step2()
        ring_r.issue()

    @pl.when(is_left)
    def _():
        ang_copy(parity).start()
        for c in range(4):
            l_over_y(0, c).start()
        ring_l.issue()
        for c in range(2):
            over_y(rwa, Y_RW, c, 2).wait_recv()
            ring_rwa.issue_chunk(c)
        all_trig()
        ring_rwa.step1()
        ring_l.step1()
        for c in range(2):
            l_over_y(1, c).start()
            l_over_y(2, c + 2).start()
        ring_rwa.step2()
        ring_rwa.step3()
        ring_rwa.finish(B0, BM, BP, BX)
        rows_of_s(rwa, sa_)
        ring_sa.issue()
        ring_l.step2()
        for c in range(2):
            l_over_y(1, c + 2).start()
            l_over_y(2, c).start()
        for c in (0, 2):
            over_y(sb_, Y_SB, c, 4).wait_recv()
            ring_sb.issue_chunk(c)
        ring_sa.step1()
        for c in (1, 3):
            over_y(sb_, Y_SB, c, 4).wait_recv()
            ring_sb.issue_chunk(c)
        ring_sa.step2()
        ring_sb.step1()
        ring_sa.step3()
        ring_l.step3()
        for c in range(4):
            l_over_y(3, c).start()

    cut = width // 2

    def add_gram(where, first=False):
        two = pl.ds(pl.multiple_of(2 * half * where, 2 * half), 2 * half)
        pair = split(above(*(beside(sa_[s, two, :], sb_[s, two, :]) for s in range(2))))
        right = tuple(n[:, cut:] for n in pair)
        top = dot3(tuple(n[:, :cut] for n in pair), pair, ((0,), (0,)))
        low = dot3(right, right, ((0,), (0,)))
        if first:
            zf[:cut, :] = top
            zf[cut:, cut:] = low
        else:
            zf[:cut, :] += top
            zf[cut:, cut:] += low

    def finish_s(*kinds):
        ring_sa.finish(*kinds)
        ring_sb.finish(*kinds)

    finish_s(B0)
    add_gram(place, first=True)

    @pl.when(is_right)
    def _():
        ring_sb.step3()

    @pl.when(is_left)
    def _():
        ring_sb.step2()

    finish_s(BM, BP)
    add_gram(minus)
    add_gram(plus)

    @pl.when(is_right)
    def _():
        ring_sa.step3()

    @pl.when(is_left)
    def _():
        ring_sb.step3()

    finish_s(BX)
    add_gram(across)
    zf[cut:, :cut] = zf[:cut, cut:].T
    gram = zf[...]
    scale = jnp.sqrt(jnp.sum(gram * gram, keepdims=True).reshape(1, 1) + 1e-06)
    zf[...] = gram / scale
    at_row = lax.broadcasted_iota(jnp.int32, (2 * half, width), 0)
    at_col = lax.broadcasted_iota(jnp.int32, (2 * half, width), 1)
    unit = jnp.where((at_col == at_row + half * row) & (at_row < half), 1.0, 0.0).astype(F32)
    mine = above(*(beside(sa_[s, own, :], sb_[s, own, :]) for s in range(2)))
    xbuf[...] = jnp.where(is_left, mine, unit)

    def refine(step, carry):
        z, x = zf[...], xbuf[...]
        z2, x2 = split(z), split(x)
        zr = tuple(n[:, cut:] for n in z2)
        both = dot3(tuple(above(a[:cut], b) for a, b in zip(z2, x2)), z2)
        top, moved = both[:cut], both[cut:]
        low = dot3(tuple(n[cut:] for n in z2), zr)
        xbuf[...] = 1.5 * x - 0.5 * moved
        top2, low2 = split(top), split(low)
        under = tuple(beside(a[:, cut:].T, b) for a, b in zip(top2, low2))
        new_top = 2.25 * z[:cut] - 1.5 * top + 0.25 * dot3(top2, z2)
        new_low = 2.25 * z[cut:, cut:] - 1.5 * low + 0.25 * dot3(under, zr)
        zf[:cut, :] = new_top
        zf[cut:, :cut] = new_top[:, cut:].T
        zf[cut:, cut:] = new_low

        @pl.when(is_right & (step == 0))
        def _():
            ring_r.step1()
            for n, kind in ((1, BM), (2, BP)):
                for c in range(4):
                    l_over_y(n, c).wait_recv()
                chip_l.share(kind)

        @pl.when(is_right & (step == 1))
        def _():
            ring_r.step2()

        @pl.when(is_right & (step == ITERS - 3))
        def _():
            ring_r.step3()
            for c in range(4):
                l_over_y(3, c).wait_recv()
            chip_l.share(BX)

        return carry

    lax.fori_loop(0, ITERS - 2, refine, 0)
    z2, x = split(zf[...]), xbuf[...]

    def times_z(rows_):
        return dot3(split(rows_), z2)

    moved = times_z(x)
    x = 1.5 * x - 0.5 * moved
    turned = 1.5 * moved - 0.5 * times_z(moved)
    for _ in range(2):
        turned = 1.5 * turned - 0.5 * times_z(turned)
    x = 1.5 * x - 0.5 * turned

    gain = jnp.sqrt(2.0 * width / scale)

    @pl.when(is_left)
    def _():
        obuf[...] = (x * gain).reshape(2, half, width)

    @pl.when(is_right)
    def _():
        chip_l.finish(B0, BM, BP, BX)
        ring_r.finish(B0, BM, BP, BX)
        ca, sa, cj, sj, cb, sb = (scalar(n) for n in range(6))
        cols = split(x[:half] * gain)
        e0, e1 = (
            dot3(cols, split(beside(sa_[s], sb_[s])), ((1,), (1,))) for s in range(2)
        )
        f, g = ca * e0 + sa * e1, ca * e1 - sa * e0
        lhs = above(beside(cj * f, cj * g), beside(-sj * g, sj * f))
        both = dot3(split(lhs), split(lbuf[...].reshape(2 * width, width)))
        c0, c1 = both[:half], both[half:]
        lhs = above(
            beside(cb * c0 - sb * c1, cb * c1 - sb * c0),
            beside(sb * c0 + cb * c1, cb * c0 + sb * c1),
        )
        right = dot3(split(lhs), split(raw[...].reshape(2 * width, width)))
        obuf[...] = (right * (1.0 / (2.0 * width))).reshape(2, half, width)

    stores = [
        pltpu.make_async_copy(obuf.at[s], out.at[0, :, s], loc.at[s]) for s in range(2)
    ]
    for store in stores:
        store.start()

    ang_copy(parity).wait_send()
    ring_rwa.drain()
    ring_sa.drain()
    ring_sb.drain()

    @pl.when(is_left)
    def _():
        for c in range(4):
            for n in range(4):
                l_over_y(n, c).wait_send()
        ring_l.drain((RP, RM, FW))

    @pl.when(is_right)
    def _():
        for c in range(2):
            over_y(rwa, Y_RW, c, 2).wait_send()
        for c in range(4):
            over_y(sb_, Y_SB, c, 4).wait_send()
        ring_rwb.drain()
        ring_r.drain()
        chip_l.drain((B0, BM, BP, BX))

    for store in stores:
        store.wait()


def per_device(sites, angles, sketch):
    half, width = sites.shape[1], sites.shape[3]
    dma, vmem = pltpu.SemaphoreType.DMA, pltpu.VMEM
    return pl.pallas_call(
        kernel,
        out_shape=jax.ShapeDtypeStruct(sites.shape, F32),
        in_specs=[
            pl.BlockSpec(memory_space=pl.ANY),
            pl.BlockSpec(memory_space=pltpu.SMEM),
            pl.BlockSpec(memory_space=pl.ANY),
        ],
        out_specs=pl.BlockSpec(memory_space=pl.ANY),
        scratch_shapes=[
            vmem((2, width, width), F32),
            vmem((2, width, width), F32),
            vmem((2, width, CUT), F32),
            vmem((2, width, width - CUT), F32),
            vmem((2, width, CUT), F32),
            vmem((2, width, width - CUT), F32),
            vmem((2 * width, width), F32),
            vmem((2 * width, width), BF16),
            vmem((2 * width, width), BF16),
            vmem((width, width), F32),
            vmem((2 * half, width), F32),
            vmem((2, half, width), F32),
            vmem((2, 16, 128), F32),
            vmem((6, 8, 128), F32),
            dma((6, 7, 4)), dma((6, 7, 4)),
            dma((7, 4)), dma((7, 4)),
            dma((3,)),
        ],
        compiler_params=pltpu.CompilerParams(
            collective_id=0, has_side_effects=True, vmem_limit_bytes=56 * 2**20
        ),
        cost_estimate=pl.CostEstimate(
            flops=20 * 6 * width**3, bytes_accessed=3 * 2**20, transcendentals=0
        ),
    )(sites, angles, sketch)


def solution(mesh):
    in_specs = (P("chain", "rows", None, None), P("chain", None), P())
    out_specs = P("chain", "rows", None, None)
    return jax.shard_map(
        per_device, mesh=mesh, in_specs=in_specs, out_specs=out_specs, check_vma=False
    )
```

```python
import functools

import jax
import jax.numpy as jnp
from jax import lax
from jax.experimental import pallas as pl
from jax.experimental.pallas import tpu as pltpu
from jax.sharding import PartitionSpec as P

ITERS = 6
MESH = pl.DeviceIdType.MESH
F32 = jnp.float32
BF16 = jnp.bfloat16

RP, RM, FW, B0, BM, BP, BX = range(7)
G_RW, G_S, G_R, G_L = range(4)
Y_S, Y_ANG, Y_L = range(3)


def split(x):
    high = x.astype(BF16)
    return high, (x - high.astype(F32)).astype(BF16)


def dot3(a, b, contract=((1,), (0,))):
    ah, al = a
    bh, bl = b
    d = functools.partial(
        lax.dot_general, dimension_numbers=(contract, ((), ())), preferred_element_type=F32
    )
    return d(ah, bh) + (d(ah, bl) + d(al, bh))


def beside(*parts):
    return jnp.concatenate(parts, 1)


def above(*parts):
    return jnp.concatenate(parts, 0)


def kernel(
    sites, angles, sketch, out,
    raw, lbuf, rw, sbuf, wbuf, wh, wl, zf, xbuf, obuf, ang, trig,
    ss, rs, vs, vr, loc, ready,
):
    chain = lax.axis_index("chain")
    row = lax.axis_index("rows")
    parity = lax.rem(chain, 2)
    core = lax.rem(row, 2)
    place = lax.div(row, 2)
    half, width = sites.shape[1], sites.shape[3]
    xs = lax.axis_size("rows") // 2
    is_left, is_right = parity == 0, parity == 1

    def at(step):
        return lax.rem(place + step + xs, xs)

    plus, minus, across = at(1), at(-1), at(2)
    dev_plus = (chain, 2 * plus + core)
    dev_minus = (chain, 2 * minus + core)
    dev_sib = (chain, 2 * place + 1 - core)
    dev_y = (chain + 1 - 2 * parity, row)

    barrier = pltpu.get_barrier_semaphore()
    for device in (dev_plus, dev_minus, dev_sib):
        pl.semaphore_signal(barrier, inc=1, device_id=device, device_id_type=MESH)

    @pl.when(is_right)
    def _():
        pl.semaphore_signal(barrier, inc=1, device_id=dev_y, device_id_type=MESH)

    def rows(block):
        return pl.ds(pl.multiple_of(half * block, half), half)

    own = rows(row)

    def chunk(view, block, c, count):
        part = 2 * half // count
        start = half * block + part * (c % (count // 2))
        return view.at[c // (count // 2), pl.ds(pl.multiple_of(start, part), part)]

    def remote(ref, send, recv, device):
        return pltpu.make_async_remote_copy(
            src_ref=ref, dst_ref=ref, send_sem=send, recv_sem=recv,
            device_id=device, device_id_type=MESH,
        )

    blk_minus, blk_plus, blk_across = (2 * n + core for n in (minus, plus, across))
    sib_own, sib_minus, sib_plus, sib_across = (
        2 * n + 1 - core for n in (place, minus, plus, across)
    )
    sends = {
        RP: (row, dev_plus), RM: (row, dev_minus), B0: (row, dev_sib),
        BM: (blk_minus, dev_sib), BP: (blk_plus, dev_sib), BX: (blk_across, dev_sib),
    }
    gets = {
        RP: blk_minus, RM: blk_plus, FW: blk_across,
        B0: sib_own, BM: sib_minus, BP: sib_plus, BX: sib_across,
    }

    class Ring:
        def __init__(self, view, which, count, shared=True):
            self.view, self.which, self.count, self.shared = view, which, count, shared
            self.low, self.high = range(count // 2), range(count // 2, count)

        def copy(self, kind, c, block, device):
            ref = chunk(self.view, block, c, self.count)
            return remote(ref, ss.at[self.which, kind, c], rs.at[self.which, kind, c], device)

        def sent(self, kind, c):
            if kind == FW:
                passed = (blk_minus, dev_plus) if c in self.low else (blk_plus, dev_minus)
                return self.copy(FW, c, *passed)
            return self.copy(kind, c, *sends[kind])

        def send(self, kind, c):
            self.sent(kind, c).start()

        def get(self, kind, c):
            self.copy(kind, c, gets[kind], dev_sib).wait_recv()

        def issue(self):
            for c, d in zip(self.low, self.high):
                self.send(RP, c)
                self.send(RM, d)
            for c, d in zip(self.low, self.high):
                self.send(RP, d)
                self.send(RM, c)
            self.share(B0)

        def share(self, kind):
            if self.shared:
                for c in range(self.count):
                    self.send(kind, c)

        def issue_chunk(self, c):
            for kind in (RP, RM, B0):
                self.send(kind, c)

        def step1(self):
            for c, d in zip(self.low, self.high):
                self.get(RP, c)
                self.send(FW, c)
                self.get(RM, d)
                self.send(FW, d)
                if self.shared:
                    self.send(BM, c)
                    self.send(BP, d)

        def step2(self):
            for c, d in zip(self.low, self.high):
                self.get(RP, d)
                self.get(RM, c)
                if self.shared:
                    self.send(BM, d)
                    self.send(BP, c)

        def step3(self):
            for c, d in zip(self.low, self.high):
                for n in (c, d):
                    self.get(FW, n)
                    if self.shared:
                        self.send(BX, n)

        def finish(self, *kinds):
            for kind in kinds:
                for c in range(self.count):
                    self.get(kind, c)

        def drain(self, kinds=range(7)):
            for kind in kinds:
                for c in range(self.count):
                    self.sent(kind, c).wait_send()

    ring_rw, ring_s = Ring(rw, G_RW, 4), Ring(sbuf, G_S, 4)
    ring_r, ring_l = Ring(raw, G_R, 4), Ring(lbuf, G_L, 4, shared=False)
    chip_l = Ring(lbuf, G_L, 4)

    def over_y(view, which, c, count, block=row):
        return remote(chunk(view, block, c, count), vs.at[which, c], vr.at[which, c], dev_y)

    l_blocks = (row, blk_minus, blk_plus, blk_across)

    def l_over_y(n, c):
        return over_y(lbuf, Y_L + n, c, 4, l_blocks[n])

    def ang_copy():
        return remote(ang.at[0], vs.at[Y_ANG, 0], vr.at[Y_ANG, 0], dev_y)

    def load_sites(view):
        copies = [
            pltpu.make_async_copy(sites.at[0, :, s], view.at[s, own], loc.at[s]) for s in range(2)
        ]
        for copy in copies:
            copy.start()
        for copy in copies:
            copy.wait()

    for n in range(2):
        ang[parity, 8 * n : 8 * n + 8, :] = jnp.full((8, 128), angles[0, n], F32)

    def scalar(n):
        return trig[n, 0:1, 0:1]

    @pl.when(is_left)
    def _():
        load_sites(lbuf)

    @pl.when(is_right)
    def _():
        fetch = pltpu.make_async_copy(sketch, wbuf, loc.at[2])
        fetch.start()
        load_sites(raw)
        kick = ang[1, 0:8, :]
        trig[4] = jnp.cos(kick)
        trig[5] = jnp.sin(kick)
        cb, sb = scalar(4), scalar(5)
        r0, r1 = raw[0, own, :], raw[1, own, :]
        mixed = above(
            beside(cb * r0 - sb * r1, sb * r0 + cb * r1),
            beside(cb * r1 - sb * r0, cb * r0 + sb * r1),
        )
        fetch.wait()
        high, low = split(wbuf[...])
        wh[...] = high
        wl[...] = low
        result = dot3(split(mixed), (wh[...], wl[...]))
        for m in range(2):
            rw[m, own, :] = result[half * m : half * (m + 1)]

    @pl.when(is_left)
    def _():
        pl.semaphore_wait(barrier, 4)
        pl.semaphore_signal(ready, inc=1, device_id=dev_y, device_id_type=MESH)

    @pl.when(is_right)
    def _():
        pl.semaphore_wait(barrier, 3)

    def all_trig():
        ang_copy().wait_recv()
        kick, coupling = ang[0, 0:8, :], 0.5 * (ang[0, 8:16, :] + ang[1, 8:16, :])
        trig[0] = jnp.cos(kick)
        trig[1] = jnp.sin(kick)
        trig[2] = jnp.cos(coupling)
        trig[3] = jnp.sin(coupling)

    def rows_of_s():
        ca, sa, cj, sj = (scalar(n) for n in range(4))
        l0, l1 = lbuf[0, own, :], lbuf[1, own, :]
        p, q = ca * l0 - sa * l1, sa * l0 + ca * l1
        lhs = above(beside(cj * p, sj * q), beside(cj * q, -sj * p))
        result = dot3(split(lhs), split(rw[...].reshape(2 * width, width)))
        for s in range(2):
            sbuf[s, own, :] = result[half * s : half * (s + 1)]

    @pl.when(is_right)
    def _():
        ring_rw.issue()
        ring_rw.step1()
        ring_rw.step2()
        all_trig()
        for c in range(4):
            l_over_y(0, c).wait_recv()
        ring_rw.step3()
        ring_rw.finish(B0, BM, BP, BX)
        rows_of_s()
        pl.semaphore_wait(ready, 1)
        for c in (0, 2, 1, 3):
            over_y(sbuf, Y_S, c, 4).start()
        ring_s.issue()
        chip_l.share(B0)
        ring_s.step1()
        ring_s.step2()
        ring_r.issue()

    @pl.when(is_left)
    def _():
        ang_copy().start()
        for c in range(4):
            l_over_y(0, c).start()
        ring_l.issue()
        ring_l.step1()
        for c in range(2):
            l_over_y(1, c).start()
            l_over_y(2, c + 2).start()
        ring_l.step2()
        for c in range(2):
            l_over_y(1, c + 2).start()
            l_over_y(2, c).start()
        ring_l.step3()
        for c in range(4):
            l_over_y(3, c).start()
        for c in (0, 2, 1, 3):
            over_y(sbuf, Y_S, c, 4).wait_recv()
            ring_s.issue_chunk(c)
        ring_s.step1()
        ring_s.step2()

    cut = width // 2

    def add_gram(where, first=False):
        two = pl.ds(pl.multiple_of(2 * half * where, 2 * half), 2 * half)
        pair = split(above(sbuf[0, two, :], sbuf[1, two, :]))
        right = tuple(n[:, cut:] for n in pair)
        top = dot3(tuple(n[:, :cut] for n in pair), pair, ((0,), (0,)))
        low = dot3(right, right, ((0,), (0,)))
        if first:
            zf[:cut, :] = top
            zf[cut:, cut:] = low
        else:
            zf[:cut, :] += top
            zf[cut:, cut:] += low

    ring_s.finish(B0)
    add_gram(place, first=True)
    ring_s.finish(BM, BP)
    add_gram(minus)
    add_gram(plus)
    ring_s.step3()
    ring_s.finish(BX)
    add_gram(across)
    zf[cut:, :cut] = zf[:cut, cut:].T
    gram = zf[...]
    scale = jnp.sqrt(jnp.sum(gram * gram, keepdims=True).reshape(1, 1) + 1e-06)
    zf[...] = gram / scale
    at_row = lax.broadcasted_iota(jnp.int32, (2 * half, width), 0)
    at_col = lax.broadcasted_iota(jnp.int32, (2 * half, width), 1)
    unit = jnp.where((at_col == at_row + half * row) & (at_row < half), 1.0, 0.0).astype(F32)
    mine = above(sbuf[0, own, :], sbuf[1, own, :])
    xbuf[...] = jnp.where(is_left, mine, unit)

    def refine(step, carry):
        z, x = zf[...], xbuf[...]
        z2, x2 = split(z), split(x)
        zr = tuple(n[:, cut:] for n in z2)
        both = dot3(tuple(above(a[:cut], b) for a, b in zip(z2, x2)), z2)
        top, moved = both[:cut], both[cut:]
        low = dot3(tuple(n[cut:] for n in z2), zr)
        xbuf[...] = 1.5 * x - 0.5 * moved
        top2, low2 = split(top), split(low)
        under = tuple(beside(a[:, cut:].T, b) for a, b in zip(top2, low2))
        new_top = 2.25 * z[:cut] - 1.5 * top + 0.25 * dot3(top2, z2)
        new_low = 2.25 * z[cut:, cut:] - 1.5 * low + 0.25 * dot3(under, zr)
        zf[:cut, :] = new_top
        zf[cut:, :cut] = new_top[:, cut:].T
        zf[cut:, cut:] = new_low

        @pl.when(is_right & (step == 0))
        def _():
            ring_r.step1()
            for n, kind in ((1, BM), (2, BP)):
                for c in range(4):
                    l_over_y(n, c).wait_recv()
                chip_l.share(kind)

        @pl.when(is_right & (step == 1))
        def _():
            ring_r.step2()

        @pl.when(is_right & (step == ITERS - 3))
        def _():
            ring_r.step3()
            for c in range(4):
                l_over_y(3, c).wait_recv()
            chip_l.share(BX)

        return carry

    lax.fori_loop(0, ITERS - 2, refine, 0)
    z2, x = split(zf[...]), xbuf[...]

    def times_z(rows_):
        return dot3(split(rows_), z2)

    moved = times_z(x)
    x = 1.5 * x - 0.5 * moved
    turned = 1.5 * moved - 0.5 * times_z(moved)
    for _ in range(2):
        turned = 1.5 * turned - 0.5 * times_z(turned)
    x = 1.5 * x - 0.5 * turned

    gain = jnp.sqrt(2.0 * width / scale)

    @pl.when(is_left)
    def _():
        obuf[...] = (x * gain).reshape(2, half, width)

    @pl.when(is_right)
    def _():
        chip_l.finish(B0, BM, BP, BX)
        ring_r.finish(B0, BM, BP, BX)
        ca, sa, cj, sj, cb, sb = (scalar(n) for n in range(6))
        cols = split(x[:half] * gain)
        e0, e1 = (
            dot3(cols, split(sbuf[s]), ((1,), (1,))) for s in range(2)
        )
        f, g = ca * e0 + sa * e1, ca * e1 - sa * e0
        lhs = above(beside(cj * f, cj * g), beside(-sj * g, sj * f))
        both = dot3(split(lhs), split(lbuf[...].reshape(2 * width, width)))
        c0, c1 = both[:half], both[half:]
        lhs = above(
            beside(cb * c0 - sb * c1, cb * c1 - sb * c0),
            beside(sb * c0 + cb * c1, cb * c0 + sb * c1),
        )
        right = dot3(split(lhs), split(raw[...].reshape(2 * width, width)))
        obuf[...] = (right * (1.0 / (2.0 * width))).reshape(2, half, width)

    stores = [
        pltpu.make_async_copy(obuf.at[s], out.at[0, :, s], loc.at[s]) for s in range(2)
    ]
    for store in stores:
        store.start()

    ring_s.drain()

    @pl.when(is_left)
    def _():
        ang_copy().wait_send()
        for c in range(4):
            for n in range(4):
                l_over_y(n, c).wait_send()
        ring_l.drain((RP, RM, FW))

    @pl.when(is_right)
    def _():
        for c in range(4):
            over_y(sbuf, Y_S, c, 4).wait_send()
        ring_rw.drain()
        ring_r.drain()
        chip_l.drain((B0, BM, BP, BX))

    for store in stores:
        store.wait()


def per_device(sites, angles, sketch):
    half, width = sites.shape[1], sites.shape[3]
    dma, vmem = pltpu.SemaphoreType.DMA, pltpu.VMEM
    return pl.pallas_call(
        kernel,
        out_shape=jax.ShapeDtypeStruct(sites.shape, F32),
        in_specs=[
            pl.BlockSpec(memory_space=pl.ANY),
            pl.BlockSpec(memory_space=pltpu.SMEM),
            pl.BlockSpec(memory_space=pl.ANY),
        ],
        out_specs=pl.BlockSpec(memory_space=pl.ANY),
        scratch_shapes=[
            vmem((2, width, width), F32),
            vmem((2, width, width), F32),
            vmem((2, width, width), F32),
            vmem((2, width, width), F32),
            vmem((2 * width, width), F32),
            vmem((2 * width, width), BF16),
            vmem((2 * width, width), BF16),
            vmem((width, width), F32),
            vmem((2 * half, width), F32),
            vmem((2, half, width), F32),
            vmem((2, 16, 128), F32),
            vmem((6, 8, 128), F32),
            dma((4, 7, 4)), dma((4, 7, 4)),
            dma((6, 4)), dma((6, 4)),
            dma((3,)), pltpu.SemaphoreType.REGULAR,
        ],
        compiler_params=pltpu.CompilerParams(
            collective_id=0, has_side_effects=True, vmem_limit_bytes=56 * 2**20
        ),
        cost_estimate=pl.CostEstimate(
            flops=20 * 6 * width**3, bytes_accessed=3 * 2**20, transcendentals=0
        ),
    )(sites, angles, sketch)


def solution(mesh):
    in_specs = (P("chain", "rows", None, None), P("chain", None), P())
    out_specs = P("chain", "rows", None, None)
    return jax.shard_map(
        per_device, mesh=mesh, in_specs=in_specs, out_specs=out_specs, check_vma=False
    )
```

```python
import functools

import jax
import jax.numpy as jnp
from jax import lax
from jax.experimental import pallas as pl
from jax.experimental.pallas import tpu as pltpu
from jax.sharding import PartitionSpec as P

ITERS = 6
MESH = pl.DeviceIdType.MESH
F32 = jnp.float32
BF16 = jnp.bfloat16

CHUNKS = 4
LOW, HIGH = (0, 1), (2, 3)
RP, RM, FW, B0, BM, BP, BX = range(7)
G_RW, G_S, G_R, G_L = range(4)
Y_S, Y_ANG, Y_L = range(3)


def split(x):
    high = x.astype(BF16)
    return high, (x - high.astype(F32)).astype(BF16)


def dot3(a, b, contract=((1,), (0,))):
    ah, al = a
    bh, bl = b
    d = functools.partial(
        lax.dot_general, dimension_numbers=(contract, ((), ())), preferred_element_type=F32
    )
    return d(ah, bh) + (d(ah, bl) + d(al, bh))


def beside(*parts):
    return jnp.concatenate(parts, 1)


def above(*parts):
    return jnp.concatenate(parts, 0)


def kernel(
    sites, angles, sketch, out,
    raw, lbuf, rw, sbuf, wbuf, wh, wl, zf, xbuf, obuf, ang, trig,
    ss, rs, vs, vr, loc, ready,
):
    chain = lax.axis_index("chain")
    row = lax.axis_index("rows")
    parity = lax.rem(chain, 2)
    core = lax.rem(row, 2)
    place = lax.div(row, 2)
    half, width = sites.shape[1], sites.shape[3]
    xs = lax.axis_size("rows") // 2
    is_left, is_right = parity == 0, parity == 1

    def at(step):
        return lax.rem(place + step + xs, xs)

    plus, minus, across = at(1), at(-1), at(2)
    dev_plus = (chain, 2 * plus + core)
    dev_minus = (chain, 2 * minus + core)
    dev_sib = (chain, 2 * place + 1 - core)
    dev_y = (chain + 1 - 2 * parity, row)

    barrier = pltpu.get_barrier_semaphore()
    for device in (dev_plus, dev_minus, dev_sib):
        pl.semaphore_signal(barrier, inc=1, device_id=device, device_id_type=MESH)

    @pl.when(is_right)
    def _():
        pl.semaphore_signal(barrier, inc=1, device_id=dev_y, device_id_type=MESH)

    def rows(block):
        return pl.ds(pl.multiple_of(half * block, half), half)

    own = rows(row)

    def chunk(view, block, c, count):
        part = 2 * half // count
        start = half * block + part * (c % (count // 2))
        return view.at[c // (count // 2), pl.ds(pl.multiple_of(start, part), part)]

    def remote(ref, send, recv, device):
        return pltpu.make_async_remote_copy(
            src_ref=ref, dst_ref=ref, send_sem=send, recv_sem=recv,
            device_id=device, device_id_type=MESH,
        )

    blk_minus, blk_plus, blk_across = (2 * n + core for n in (minus, plus, across))
    sib_own, sib_minus, sib_plus, sib_across = (
        2 * n + 1 - core for n in (place, minus, plus, across)
    )
    sends = {
        RP: (row, dev_plus), RM: (row, dev_minus), B0: (row, dev_sib),
        BM: (blk_minus, dev_sib), BP: (blk_plus, dev_sib), BX: (blk_across, dev_sib),
    }
    gets = {
        RP: blk_minus, RM: blk_plus, FW: blk_across,
        B0: sib_own, BM: sib_minus, BP: sib_plus, BX: sib_across,
    }

    class Ring:
        def __init__(self, view, which, shared=True):
            self.view, self.which, self.shared = view, which, shared

        def copy(self, kind, c, block, device):
            ref = chunk(self.view, block, c, CHUNKS)
            return remote(ref, ss.at[self.which], rs.at[self.which, kind, c], device)

        def send(self, kind, c):
            if kind == FW:
                passed = (blk_minus, dev_plus) if c in LOW else (blk_plus, dev_minus)
                self.copy(FW, c, *passed).start()
            else:
                self.copy(kind, c, *sends[kind]).start()

        def get(self, kind, c):
            self.copy(kind, c, gets[kind], dev_sib).wait_recv()

        def whole(self, kind, block):
            ref = self.view.at[:, rows(block)]
            return remote(ref, ss.at[self.which], rs.at[self.which, kind, 0], dev_sib)

        def share(self, kind):
            if self.shared:
                self.whole(kind, sends[kind][0]).start()

        def issue(self):
            for c, d in zip(LOW, HIGH):
                self.send(RP, c)
                self.send(RM, d)
            for c, d in zip(LOW, HIGH):
                self.send(RP, d)
                self.send(RM, c)
            self.share(B0)

        def issue_chunk(self, c):
            self.send(RP, c)
            self.send(RM, c)

        def step1(self):
            for c, d in zip(LOW, HIGH):
                self.get(RP, c)
                self.send(FW, c)
                self.get(RM, d)
                self.send(FW, d)

        def step2(self):
            for c in HIGH:
                self.get(RP, c)
            self.share(BM)
            for c in LOW:
                self.get(RM, c)
            self.share(BP)

        def step3(self):
            for c, d in zip(LOW, HIGH):
                for n in (c, d):
                    self.get(FW, n)
                    if self.shared:
                        ref = chunk(self.view, blk_across, n, CHUNKS)
                        remote(ref, ss.at[self.which], rs.at[self.which, BX, 0], dev_sib).start()

        def finish(self, *kinds):
            for kind in kinds:
                self.whole(kind, gets[kind]).wait_recv()

        def drain(self, blocks):
            ref = self.view.at[:, pl.ds(0, half * blocks)]
            remote(ref, ss.at[self.which], rs.at[self.which, RP, 0], dev_sib).wait_send()

    ring_rw, ring_s = Ring(rw, G_RW), Ring(sbuf, G_S)
    ring_r, ring_l = Ring(raw, G_R), Ring(lbuf, G_L, shared=False)
    chip_l = Ring(lbuf, G_L)

    def over_y(view, which, c, count, block=row):
        return remote(chunk(view, block, c, count), vs.at[which], vr.at[which, c], dev_y)

    l_blocks = (row, blk_minus, blk_plus, blk_across)

    def l_over_y(n, c):
        ref = chunk(lbuf, l_blocks[n], c, 4)
        return remote(ref, vs.at[Y_L], vr.at[Y_L + n, c], dev_y)

    def y_drain(view, which, blocks):
        ref = view.at[:, pl.ds(0, half * blocks)]
        remote(ref, vs.at[which], vr.at[which, 0], dev_y).wait_send()

    def ang_copy():
        return remote(ang.at[0], vs.at[Y_ANG], vr.at[Y_ANG, 0], dev_y)

    def load_sites(view):
        copies = [
            pltpu.make_async_copy(sites.at[0, :, s], view.at[s, own], loc.at[s]) for s in range(2)
        ]
        for copy in copies:
            copy.start()
        for copy in copies:
            copy.wait()

    for n in range(2):
        ang[parity, 8 * n : 8 * n + 8, :] = jnp.full((8, 128), angles[0, n], F32)

    def scalar(n):
        return trig[n, 0:1, 0:1]

    @pl.when(is_left)
    def _():
        load_sites(lbuf)

    @pl.when(is_right)
    def _():
        fetch = pltpu.make_async_copy(sketch, wbuf, loc.at[2])
        fetch.start()
        load_sites(raw)
        kick = ang[1, 0:8, :]
        trig[4] = jnp.cos(kick)
        trig[5] = jnp.sin(kick)
        cb, sb = scalar(4), scalar(5)
        r0, r1 = raw[0, own, :], raw[1, own, :]
        mixed = above(
            beside(cb * r0 - sb * r1, sb * r0 + cb * r1),
            beside(cb * r1 - sb * r0, cb * r0 + sb * r1),
        )
        fetch.wait()
        high, low = split(wbuf[...])
        wh[...] = high
        wl[...] = low
        result = dot3(split(mixed), (wh[...], wl[...]))
        for m in range(2):
            rw[m, own, :] = result[half * m : half * (m + 1)]

    @pl.when(is_left)
    def _():
        pl.semaphore_wait(barrier, 4)
        pl.semaphore_signal(ready, inc=1, device_id=dev_y, device_id_type=MESH)

    @pl.when(is_right)
    def _():
        pl.semaphore_wait(barrier, 3)

    def all_trig():
        ang_copy().wait_recv()
        kick, coupling = ang[0, 0:8, :], 0.5 * (ang[0, 8:16, :] + ang[1, 8:16, :])
        trig[0] = jnp.cos(kick)
        trig[1] = jnp.sin(kick)
        trig[2] = jnp.cos(coupling)
        trig[3] = jnp.sin(coupling)

    def rows_of_s():
        ca, sa, cj, sj = (scalar(n) for n in range(4))
        l0, l1 = lbuf[0, own, :], lbuf[1, own, :]
        p, q = ca * l0 - sa * l1, sa * l0 + ca * l1
        lhs = above(beside(cj * p, sj * q), beside(cj * q, -sj * p))
        result = dot3(split(lhs), split(rw[...].reshape(2 * width, width)))
        for s in range(2):
            sbuf[s, own, :] = result[half * s : half * (s + 1)]

    @pl.when(is_right)
    def _():
        ring_rw.issue()
        ring_rw.step1()
        ring_rw.step2()
        all_trig()
        for c in range(4):
            l_over_y(0, c).wait_recv()
        ring_rw.step3()
        ring_rw.finish(B0, BM, BP, BX)
        rows_of_s()
        pl.semaphore_wait(ready, 1)
        for c in (0, 2, 1, 3):
            over_y(sbuf, Y_S, c, 4).start()
        ring_s.issue()
        chip_l.share(B0)
        ring_s.step1()
        ring_s.step2()
        ring_r.issue()

    @pl.when(is_left)
    def _():
        ang_copy().start()
        for c in range(4):
            l_over_y(0, c).start()
        ring_l.issue()
        ring_l.step1()
        for c in range(2):
            l_over_y(1, c).start()
            l_over_y(2, c + 2).start()
        ring_l.step2()
        for c in range(2):
            l_over_y(1, c + 2).start()
            l_over_y(2, c).start()
        ring_l.step3()
        for c in range(4):
            l_over_y(3, c).start()
        for c in (0, 2, 1, 3):
            over_y(sbuf, Y_S, c, 4).wait_recv()
            ring_s.issue_chunk(c)
        ring_s.share(B0)
        ring_s.step1()
        ring_s.step2()

    cut = width // 2

    def add_gram(where, first=False):
        two = pl.ds(pl.multiple_of(2 * half * where, 2 * half), 2 * half)
        pair = split(above(sbuf[0, two, :], sbuf[1, two, :]))
        right = tuple(n[:, cut:] for n in pair)
        top = dot3(tuple(n[:, :cut] for n in pair), pair, ((0,), (0,)))
        low = dot3(right, right, ((0,), (0,)))
        if first:
            zf[:cut, :] = top
            zf[cut:, cut:] = low
        else:
            zf[:cut, :] += top
            zf[cut:, cut:] += low

    ring_s.finish(B0)
    add_gram(place, first=True)
    ring_s.finish(BM, BP)
    add_gram(minus)
    add_gram(plus)
    ring_s.step3()
    ring_s.finish(BX)
    add_gram(across)
    zf[cut:, :cut] = zf[:cut, cut:].T
    gram = zf[...]
    scale = jnp.sqrt(jnp.sum(gram * gram, keepdims=True).reshape(1, 1) + 1e-06)
    zf[...] = gram / scale
    at_row = lax.broadcasted_iota(jnp.int32, (2 * half, width), 0)
    at_col = lax.broadcasted_iota(jnp.int32, (2 * half, width), 1)
    unit = jnp.where((at_col == at_row + half * row) & (at_row < half), 1.0, 0.0).astype(F32)
    mine = above(sbuf[0, own, :], sbuf[1, own, :])
    xbuf[...] = jnp.where(is_left, mine, unit)

    def refine(step, carry):
        z, x = zf[...], xbuf[...]
        z2, x2 = split(z), split(x)
        zr = tuple(n[:, cut:] for n in z2)
        both = dot3(tuple(above(a[:cut], b) for a, b in zip(z2, x2)), z2)
        top, moved = both[:cut], both[cut:]
        low = dot3(tuple(n[cut:] for n in z2), zr)
        xbuf[...] = 1.5 * x - 0.5 * moved
        top2, low2 = split(top), split(low)
        under = tuple(beside(a[:, cut:].T, b) for a, b in zip(top2, low2))
        new_top = 2.25 * z[:cut] - 1.5 * top + 0.25 * dot3(top2, z2)
        new_low = 2.25 * z[cut:, cut:] - 1.5 * low + 0.25 * dot3(under, zr)
        zf[:cut, :] = new_top
        zf[cut:, :cut] = new_top[:, cut:].T
        zf[cut:, cut:] = new_low

        @pl.when(is_right & (step == 0))
        def _():
            ring_r.step1()
            for n, kind in ((1, BM), (2, BP)):
                for c in range(4):
                    l_over_y(n, c).wait_recv()
                chip_l.share(kind)

        @pl.when(is_right & (step == 1))
        def _():
            ring_r.step2()

        @pl.when(is_right & (step == ITERS - 3))
        def _():
            ring_r.step3()
            for c in range(4):
                l_over_y(3, c).wait_recv()
            chip_l.share(BX)

        return carry

    lax.fori_loop(0, ITERS - 2, refine, 0)
    z2, x = split(zf[...]), xbuf[...]

    def times_z(rows_):
        return dot3(split(rows_), z2)

    moved = times_z(x)
    x = 1.5 * x - 0.5 * moved
    turned = 1.5 * moved - 0.5 * times_z(moved)
    for _ in range(2):
        turned = 1.5 * turned - 0.5 * times_z(turned)
    x = 1.5 * x - 0.5 * turned

    gain = jnp.sqrt(2.0 * width / scale)

    @pl.when(is_left)
    def _():
        obuf[...] = (x * gain).reshape(2, half, width)

    @pl.when(is_right)
    def _():
        chip_l.finish(B0, BM, BP, BX)
        ring_r.finish(B0, BM, BP, BX)
        ca, sa, cj, sj, cb, sb = (scalar(n) for n in range(6))
        cols = split(x[:half] * gain)
        e0, e1 = (
            dot3(cols, split(sbuf[s]), ((1,), (1,))) for s in range(2)
        )
        f, g = ca * e0 + sa * e1, ca * e1 - sa * e0
        lhs = above(beside(cj * f, cj * g), beside(-sj * g, sj * f))
        both = dot3(split(lhs), split(lbuf[...].reshape(2 * width, width)))
        c0, c1 = both[:half], both[half:]
        lhs = above(
            beside(cb * c0 - sb * c1, cb * c1 - sb * c0),
            beside(sb * c0 + cb * c1, cb * c0 + sb * c1),
        )
        right = dot3(split(lhs), split(raw[...].reshape(2 * width, width)))
        obuf[...] = (right * (1.0 / (2.0 * width))).reshape(2, half, width)

    stores = [
        pltpu.make_async_copy(obuf.at[s], out.at[0, :, s], loc.at[s]) for s in range(2)
    ]
    for store in stores:
        store.start()

    ring_s.drain(7)

    @pl.when(is_left)
    def _():
        ang_copy().wait_send()
        y_drain(lbuf, Y_L, 4)
        ring_l.drain(3)

    @pl.when(is_right)
    def _():
        y_drain(sbuf, Y_S, 1)
        ring_rw.drain(7)
        ring_r.drain(7)
        chip_l.drain(4)

    for store in stores:
        store.wait()


def per_device(sites, angles, sketch):
    half, width = sites.shape[1], sites.shape[3]
    dma, vmem = pltpu.SemaphoreType.DMA, pltpu.VMEM
    return pl.pallas_call(
        kernel,
        out_shape=jax.ShapeDtypeStruct(sites.shape, F32),
        in_specs=[
            pl.BlockSpec(memory_space=pl.ANY),
            pl.BlockSpec(memory_space=pltpu.SMEM),
            pl.BlockSpec(memory_space=pl.ANY),
        ],
        out_specs=pl.BlockSpec(memory_space=pl.ANY),
        scratch_shapes=[
            vmem((2, width, width), F32),
            vmem((2, width, width), F32),
            vmem((2, width, width), F32),
            vmem((2, width, width), F32),
            vmem((2 * width, width), F32),
            vmem((2 * width, width), BF16),
            vmem((2 * width, width), BF16),
            vmem((width, width), F32),
            vmem((2 * half, width), F32),
            vmem((2, half, width), F32),
            vmem((2, 16, 128), F32),
            vmem((6, 8, 128), F32),
            dma((4,)), dma((4, 7, 4)),
            dma((6,)), dma((6, 4)),
            dma((3,)), pltpu.SemaphoreType.REGULAR,
        ],
        compiler_params=pltpu.CompilerParams(
            collective_id=0, has_side_effects=True, vmem_limit_bytes=56 * 2**20
        ),
        cost_estimate=pl.CostEstimate(
            flops=20 * 6 * width**3, bytes_accessed=3 * 2**20, transcendentals=0
        ),
    )(sites, angles, sketch)


def solution(mesh):
    in_specs = (P("chain", "rows", None, None), P("chain", None), P())
    out_specs = P("chain", "rows", None, None)
    return jax.shard_map(
        per_device, mesh=mesh, in_specs=in_specs, out_specs=out_specs, check_vma=False
    )
```

```python
import functools

import jax
import jax.numpy as jnp
from jax import lax
from jax.experimental import pallas as pl
from jax.experimental.pallas import tpu as pltpu
from jax.sharding import PartitionSpec as P

ITERS = 6
MESH = pl.DeviceIdType.MESH
F32 = jnp.float32
BF16 = jnp.bfloat16

CHUNKS = 4
LOW, HIGH = (0, 1), (2, 3)
RP, RM, FW, B0, BM, BP, BX = range(7)
G_RW, G_S, G_R, G_L = range(4)
Y_S, Y_ANG, Y_L = range(3)


def split(x):
    high = x.astype(BF16)
    return high, (x - high.astype(F32)).astype(BF16)


def dot3(a, b, contract=((1,), (0,))):
    ah, al = a
    bh, bl = b
    d = functools.partial(
        lax.dot_general, dimension_numbers=(contract, ((), ())), preferred_element_type=F32
    )
    return d(ah, bh) + (d(ah, bl) + d(al, bh))


def beside(*parts):
    return jnp.concatenate(parts, 1)


def above(*parts):
    return jnp.concatenate(parts, 0)


def kernel(
    sites, angles, sketch, out,
    raw, lbuf, rw, sbuf, wbuf, wh, wl, zf, xbuf, obuf, ang, trig,
    ss, rs, vs, vr, loc, ready,
):
    chain = lax.axis_index("chain")
    row = lax.axis_index("rows")
    parity = lax.rem(chain, 2)
    core = lax.rem(row, 2)
    place = lax.div(row, 2)
    half, width = sites.shape[1], sites.shape[3]
    xs = lax.axis_size("rows") // 2
    is_left, is_right = parity == 0, parity == 1

    def at(step):
        return lax.rem(place + step + xs, xs)

    plus, minus, across = at(1), at(-1), at(2)
    dev_plus = (chain, 2 * plus + core)
    dev_minus = (chain, 2 * minus + core)
    dev_sib = (chain, 2 * place + 1 - core)
    dev_y = (chain + 1 - 2 * parity, row)

    barrier = pltpu.get_barrier_semaphore()
    for device in (dev_plus, dev_minus, dev_sib):
        pl.semaphore_signal(barrier, inc=1, device_id=device, device_id_type=MESH)

    @pl.when(is_right)
    def _():
        pl.semaphore_signal(barrier, inc=1, device_id=dev_y, device_id_type=MESH)

    def rows(block):
        return pl.ds(pl.multiple_of(half * block, half), half)

    own = rows(row)

    def chunk(view, block, c, count):
        part = 2 * half // count
        start = half * block + part * (c % (count // 2))
        return view.at[c // (count // 2), pl.ds(pl.multiple_of(start, part), part)]

    def remote(ref, send, recv, device):
        return pltpu.make_async_remote_copy(
            src_ref=ref, dst_ref=ref, send_sem=send, recv_sem=recv,
            device_id=device, device_id_type=MESH,
        )

    blk_minus, blk_plus, blk_across = (2 * n + core for n in (minus, plus, across))
    sib_own, sib_minus, sib_plus, sib_across = (
        2 * n + 1 - core for n in (place, minus, plus, across)
    )
    sends = {
        RP: (row, dev_plus), RM: (row, dev_minus), B0: (row, dev_sib),
        BM: (blk_minus, dev_sib), BP: (blk_plus, dev_sib), BX: (blk_across, dev_sib),
    }
    gets = {
        RP: blk_minus, RM: blk_plus, FW: blk_across,
        B0: sib_own, BM: sib_minus, BP: sib_plus, BX: sib_across,
    }

    class Ring:
        def __init__(self, view, which, shared=True):
            self.view, self.which, self.shared = view, which, shared

        def copy(self, kind, c, block, device):
            ref = chunk(self.view, block, c, CHUNKS)
            return remote(ref, ss.at[self.which], rs.at[self.which, kind, c], device)

        def send(self, kind, c):
            if kind == FW:
                passed = (blk_minus, dev_plus) if c in LOW else (blk_plus, dev_minus)
                self.copy(FW, c, *passed).start()
            else:
                self.copy(kind, c, *sends[kind]).start()

        def get(self, kind, c):
            self.copy(kind, c, gets[kind], dev_sib).wait_recv()

        def whole(self, kind, block):
            ref = self.view.at[:, rows(block)]
            return remote(ref, ss.at[self.which], rs.at[self.which, kind, 0], dev_sib)

        def share(self, kind):
            if self.shared:
                self.whole(kind, sends[kind][0]).start()

        def issue(self):
            for c, d in zip(LOW, HIGH):
                self.send(RP, c)
                self.send(RM, d)
            for c, d in zip(LOW, HIGH):
                self.send(RP, d)
                self.send(RM, c)
            self.share(B0)

        def issue_chunk(self, c):
            self.send(RP, c)
            self.send(RM, c)

        def step1(self):
            for c, d in zip(LOW, HIGH):
                self.get(RP, c)
                self.send(FW, c)
                self.get(RM, d)
                self.send(FW, d)

        def step2(self):
            for c in HIGH:
                self.get(RP, c)
            self.share(BM)
            for c in LOW:
                self.get(RM, c)
            self.share(BP)

        def step3(self):
            for c, d in zip(LOW, HIGH):
                for n in (c, d):
                    self.get(FW, n)
                    if self.shared:
                        ref = chunk(self.view, blk_across, n, CHUNKS)
                        remote(ref, ss.at[self.which], rs.at[self.which, BX, 0], dev_sib).start()

        def finish(self, *kinds):
            for kind in kinds:
                self.whole(kind, gets[kind]).wait_recv()

        def drain(self, blocks):
            ref = self.view.at[:, pl.ds(0, half * blocks)]
            remote(ref, ss.at[self.which], rs.at[self.which, RP, 0], dev_sib).wait_send()

    ring_rw, ring_s = Ring(rw, G_RW), Ring(sbuf, G_S)
    ring_r, ring_l = Ring(raw, G_R), Ring(lbuf, G_L, shared=False)
    chip_l = Ring(lbuf, G_L)

    def over_y(view, which, c, count, block=row):
        return remote(chunk(view, block, c, count), vs.at[which], vr.at[which, c], dev_y)

    l_blocks = (row, blk_minus, blk_plus, blk_across)

    def l_over_y(n, c):
        ref = chunk(lbuf, l_blocks[n], c, 4)
        return remote(ref, vs.at[Y_L], vr.at[Y_L + n, c], dev_y)

    def y_drain(view, which, blocks):
        ref = view.at[:, pl.ds(0, half * blocks)]
        remote(ref, vs.at[which], vr.at[which, 0], dev_y).wait_send()

    def ang_copy():
        return remote(ang.at[0], vs.at[Y_ANG], vr.at[Y_ANG, 0], dev_y)

    def load_sites(view):
        copies = [
            pltpu.make_async_copy(sites.at[0, :, s], view.at[s, own], loc.at[s]) for s in range(2)
        ]
        for copy in copies:
            copy.start()
        for copy in copies:
            copy.wait()

    for n in range(2):
        ang[parity, 8 * n : 8 * n + 8, :] = jnp.full((8, 128), angles[0, n], F32)

    def scalar(n):
        return trig[n, 0:1, 0:1]

    @pl.when(is_left)
    def _():
        load_sites(lbuf)

    @pl.when(is_right)
    def _():
        fetch = pltpu.make_async_copy(sketch, wbuf, loc.at[2])
        fetch.start()
        load_sites(raw)
        kick = ang[1, 0:8, :]
        trig[4] = jnp.cos(kick)
        trig[5] = jnp.sin(kick)
        cb, sb = scalar(4), scalar(5)
        r0, r1 = raw[0, own, :], raw[1, own, :]
        mixed = above(
            beside(cb * r0 - sb * r1, sb * r0 + cb * r1),
            beside(cb * r1 - sb * r0, cb * r0 + sb * r1),
        )
        fetch.wait()
        high, low = split(wbuf[...])
        wh[...] = high
        wl[...] = low
        result = dot3(split(mixed), (wh[...], wl[...]))
        for m in range(2):
            rw[m, own, :] = result[half * m : half * (m + 1)]

    @pl.when(is_left)
    def _():
        pl.semaphore_wait(barrier, 4)
        pl.semaphore_signal(ready, inc=1, device_id=dev_y, device_id_type=MESH)

    @pl.when(is_right)
    def _():
        pl.semaphore_wait(barrier, 3)

    def all_trig():
        ang_copy().wait_recv()
        kick, coupling = ang[0, 0:8, :], 0.5 * (ang[0, 8:16, :] + ang[1, 8:16, :])
        trig[0] = jnp.cos(kick)
        trig[1] = jnp.sin(kick)
        trig[2] = jnp.cos(coupling)
        trig[3] = jnp.sin(coupling)

    def rows_of_s():
        ca, sa, cj, sj = (scalar(n) for n in range(4))
        l0, l1 = lbuf[0, own, :], lbuf[1, own, :]
        p, q = ca * l0 - sa * l1, sa * l0 + ca * l1
        lhs = above(beside(cj * p, sj * q), beside(cj * q, -sj * p))
        result = dot3(split(lhs), split(rw[...].reshape(2 * width, width)))
        for s in range(2):
            sbuf[s, own, :] = result[half * s : half * (s + 1)]

    @pl.when(is_right)
    def _():
        ring_rw.issue()
        ring_rw.step1()
        ring_rw.step2()
        all_trig()
        for c in range(4):
            l_over_y(0, c).wait_recv()
        ring_rw.step3()
        ring_rw.finish(B0, BM, BP, BX)
        rows_of_s()
        pl.semaphore_wait(ready, 1)
        for c in (0, 2, 1, 3):
            over_y(sbuf, Y_S, c, 4).start()
        ring_s.issue()
        chip_l.share(B0)
        ring_s.step1()
        ring_s.step2()
        ring_r.issue()

    @pl.when(is_left)
    def _():
        ang_copy().start()
        for c in range(4):
            l_over_y(0, c).start()
        ring_l.issue()
        ring_l.step1()
        for c in range(2):
            l_over_y(1, c).start()
            l_over_y(2, c + 2).start()
        ring_l.step2()
        for c in range(2):
            l_over_y(1, c + 2).start()
            l_over_y(2, c).start()
        ring_l.step3()
        for c in range(4):
            l_over_y(3, c).start()
        for c in (0, 2, 1, 3):
            over_y(sbuf, Y_S, c, 4).wait_recv()
            ring_s.issue_chunk(c)
        ring_s.share(B0)
        ring_s.step1()
        ring_s.step2()

    cut = width // 2

    def add_gram(where, first=False):
        two = pl.ds(pl.multiple_of(2 * half * where, 2 * half), 2 * half)
        pair = split(above(sbuf[0, two, :], sbuf[1, two, :]))
        right = tuple(n[:, cut:] for n in pair)
        top = dot3(tuple(n[:, :cut] for n in pair), pair, ((0,), (0,)))
        low = dot3(right, right, ((0,), (0,)))
        if first:
            zf[:cut, :] = top
            zf[cut:, cut:] = low
        else:
            zf[:cut, :] += top
            zf[cut:, cut:] += low

    ring_s.finish(B0)
    add_gram(place, first=True)
    ring_s.finish(BM, BP)
    add_gram(minus)
    add_gram(plus)
    ring_s.step3()
    at_row = lax.broadcasted_iota(jnp.int32, (2 * half, width), 0)
    at_col = lax.broadcasted_iota(jnp.int32, (2 * half, width), 1)
    unit = jnp.where((at_col == at_row + half * row) & (at_row < half), 1.0, 0.0).astype(F32)
    mine = above(sbuf[0, own, :], sbuf[1, own, :])
    xbuf[...] = jnp.where(is_left, mine, unit)
    ring_s.finish(BX)
    add_gram(across)
    top, low = zf[:cut, :], zf[cut:, cut:]
    squares = jnp.sum(top * top) + jnp.sum(low * low) + jnp.sum(top[:, cut:] * top[:, cut:])
    scale = jnp.sqrt(jnp.full((1, 1), squares, F32) + 1e-06)
    per = 1.0 / scale
    zf[:cut, :] = top * per
    zf[cut:, :cut] = top[:, cut:].T * per
    zf[cut:, cut:] = low * per

    def refine():
        z, x = zf[...], xbuf[...]
        z2 = split(z)
        zr = tuple(n[:, cut:] for n in z2)
        top = dot3(tuple(n[:cut] for n in z2), z2)
        low = dot3(tuple(n[cut:] for n in z2), zr)
        top2, low2 = split(top), split(low)
        under = tuple(beside(a[:, cut:].T, b) for a, b in zip(top2, low2))
        new_top = 2.25 * z[:cut] - 1.5 * top + 0.25 * dot3(top2, z2)
        new_low = 2.25 * z[cut:, cut:] - 1.5 * low + 0.25 * dot3(under, zr)
        xbuf[...] = 1.5 * x - 0.5 * dot3(split(x), z2)
        zf[:cut, :] = new_top
        zf[cut:, :cut] = new_top[:, cut:].T
        zf[cut:, cut:] = new_low

    for _ in range((ITERS - 2) // 2):
        refine()

    @pl.when(is_right)
    def _():
        ring_r.step1()
        for n, kind in ((1, BM), (2, BP)):
            for c in range(4):
                l_over_y(n, c).wait_recv()
            chip_l.share(kind)

    for _ in range((ITERS - 2) // 2):
        refine()

    @pl.when(is_right)
    def _():
        ring_r.step2()
        for c in range(4):
            l_over_y(3, c).wait_recv()
        chip_l.share(BX)
        ring_r.step3()

    z2, x = split(zf[...]), xbuf[...]

    def times_z(rows_):
        return dot3(split(rows_), z2)

    moved = times_z(x)
    x = 1.5 * x - 0.5 * moved
    turned = 1.5 * moved - 0.5 * times_z(moved)
    for _ in range(2):
        turned = 1.5 * turned - 0.5 * times_z(turned)
    x = 1.5 * x - 0.5 * turned

    gain = jnp.sqrt(2.0 * width / scale)

    @pl.when(is_left)
    def _():
        obuf[...] = (x * gain).reshape(2, half, width)

    @pl.when(is_right)
    def _():
        chip_l.finish(B0, BM, BP, BX)
        ring_r.finish(B0, BM, BP, BX)
        ca, sa, cj, sj, cb, sb = (scalar(n) for n in range(6))
        cols = split(x[:half] * gain)
        e0, e1 = (
            dot3(cols, split(sbuf[s]), ((1,), (1,))) for s in range(2)
        )
        f, g = ca * e0 + sa * e1, ca * e1 - sa * e0
        lhs = above(beside(cj * f, cj * g), beside(-sj * g, sj * f))
        both = dot3(split(lhs), split(lbuf[...].reshape(2 * width, width)))
        c0, c1 = both[:half], both[half:]
        lhs = above(
            beside(cb * c0 - sb * c1, cb * c1 - sb * c0),
            beside(sb * c0 + cb * c1, cb * c0 + sb * c1),
        )
        right = dot3(split(lhs), split(raw[...].reshape(2 * width, width)))
        obuf[...] = (right * (1.0 / (2.0 * width))).reshape(2, half, width)

    stores = [
        pltpu.make_async_copy(obuf.at[s], out.at[0, :, s], loc.at[s]) for s in range(2)
    ]
    for store in stores:
        store.start()

    ring_s.drain(7)

    @pl.when(is_left)
    def _():
        ang_copy().wait_send()
        y_drain(lbuf, Y_L, 4)
        ring_l.drain(3)

    @pl.when(is_right)
    def _():
        y_drain(sbuf, Y_S, 1)
        ring_rw.drain(7)
        ring_r.drain(7)
        chip_l.drain(4)

    for store in stores:
        store.wait()


def per_device(sites, angles, sketch):
    half, width = sites.shape[1], sites.shape[3]
    dma, vmem = pltpu.SemaphoreType.DMA, pltpu.VMEM
    return pl.pallas_call(
        kernel,
        out_shape=jax.ShapeDtypeStruct(sites.shape, F32),
        in_specs=[
            pl.BlockSpec(memory_space=pl.ANY),
            pl.BlockSpec(memory_space=pltpu.SMEM),
            pl.BlockSpec(memory_space=pl.ANY),
        ],
        out_specs=pl.BlockSpec(memory_space=pl.ANY),
        scratch_shapes=[
            vmem((2, width, width), F32),
            vmem((2, width, width), F32),
            vmem((2, width, width), F32),
            vmem((2, width, width), F32),
            vmem((2 * width, width), F32),
            vmem((2 * width, width), BF16),
            vmem((2 * width, width), BF16),
            vmem((width, width), F32),
            vmem((2 * half, width), F32),
            vmem((2, half, width), F32),
            vmem((2, 16, 128), F32),
            vmem((6, 8, 128), F32),
            dma((4,)), dma((4, 7, 4)),
            dma((6,)), dma((6, 4)),
            dma((3,)), pltpu.SemaphoreType.REGULAR,
        ],
        compiler_params=pltpu.CompilerParams(
            collective_id=0, has_side_effects=True, vmem_limit_bytes=56 * 2**20
        ),
        cost_estimate=pl.CostEstimate(
            flops=20 * 6 * width**3, bytes_accessed=3 * 2**20, transcendentals=0
        ),
    )(sites, angles, sketch)


def solution(mesh):
    in_specs = (P("chain", "rows", None, None), P("chain", None), P())
    out_specs = P("chain", "rows", None, None)
    return jax.shard_map(
        per_device, mesh=mesh, in_specs=in_specs, out_specs=out_specs, check_vma=False
    )
```

```python
import functools

import jax
import jax.numpy as jnp
from jax import lax
from jax.experimental import pallas as pl
from jax.experimental.pallas import tpu as pltpu
from jax.sharding import PartitionSpec as P

ITERS = 6
MESH = pl.DeviceIdType.MESH
F32 = jnp.float32
BF16 = jnp.bfloat16

CHUNKS = 4
LOW, HIGH = (0, 1), (2, 3)
RP, RM, FW, B0, BM, BP, BX = range(7)
G_RW, G_S, G_R, G_L = range(4)
Y_S, Y_ANG, Y_L = range(3)


def split(x):
    high = x.astype(BF16)
    return high, (x - high.astype(F32)).astype(BF16)


def dot3(a, b, contract=((1,), (0,))):
    ah, al = a
    bh, bl = b
    d = functools.partial(
        lax.dot_general, dimension_numbers=(contract, ((), ())), preferred_element_type=F32
    )
    return d(ah, bh) + (d(ah, bl) + d(al, bh))


def beside(*parts):
    return jnp.concatenate(parts, 1)


def above(*parts):
    return jnp.concatenate(parts, 0)


def rows3(a, b, contract=((1,), (0,))):
    ah, al = a
    bh, bl = b
    d = functools.partial(
        lax.dot_general, dimension_numbers=(contract, ((), ())), preferred_element_type=F32
    )
    both = d(above(ah, al), bh)
    count = ah.shape[0]
    return both[:count] + (d(ah, bl) + both[count:])


def kernel(
    sites, angles, sketch, out,
    raw, lbuf, rw, sbuf, wbuf, wh, wl, zf, xbuf, obuf, ang, trig,
    ss, rs, vs, vr, loc, ready,
):
    chain = lax.axis_index("chain")
    row = lax.axis_index("rows")
    parity = lax.rem(chain, 2)
    core = lax.rem(row, 2)
    place = lax.div(row, 2)
    half, width = sites.shape[1], sites.shape[3]
    xs = lax.axis_size("rows") // 2
    is_left, is_right = parity == 0, parity == 1

    def at(step):
        return lax.rem(place + step + xs, xs)

    plus, minus, across = at(1), at(-1), at(2)
    dev_plus = (chain, 2 * plus + core)
    dev_minus = (chain, 2 * minus + core)
    dev_sib = (chain, 2 * place + 1 - core)
    dev_y = (chain + 1 - 2 * parity, row)

    barrier = pltpu.get_barrier_semaphore()
    for device in (dev_plus, dev_minus, dev_sib):
        pl.semaphore_signal(barrier, inc=1, device_id=device, device_id_type=MESH)

    @pl.when(is_right)
    def _():
        pl.semaphore_signal(barrier, inc=1, device_id=dev_y, device_id_type=MESH)

    def rows(block):
        return pl.ds(pl.multiple_of(half * block, half), half)

    own = rows(row)

    def chunk(view, block, c, count):
        part = 2 * half // count
        start = half * block + part * (c % (count // 2))
        return view.at[c // (count // 2), pl.ds(pl.multiple_of(start, part), part)]

    def remote(ref, send, recv, device):
        return pltpu.make_async_remote_copy(
            src_ref=ref, dst_ref=ref, send_sem=send, recv_sem=recv,
            device_id=device, device_id_type=MESH,
        )

    blk_minus, blk_plus, blk_across = (2 * n + core for n in (minus, plus, across))
    sib_own, sib_minus, sib_plus, sib_across = (
        2 * n + 1 - core for n in (place, minus, plus, across)
    )
    sends = {
        RP: (row, dev_plus), RM: (row, dev_minus), B0: (row, dev_sib),
        BM: (blk_minus, dev_sib), BP: (blk_plus, dev_sib), BX: (blk_across, dev_sib),
    }
    gets = {
        RP: blk_minus, RM: blk_plus, FW: blk_across,
        B0: sib_own, BM: sib_minus, BP: sib_plus, BX: sib_across,
    }

    class Ring:
        def __init__(self, view, which, shared=True):
            self.view, self.which, self.shared = view, which, shared

        def copy(self, kind, c, block, device):
            ref = chunk(self.view, block, c, CHUNKS)
            return remote(ref, ss.at[self.which], rs.at[self.which, kind, c], device)

        def send(self, kind, c):
            if kind == FW:
                passed = (blk_minus, dev_plus) if c in LOW else (blk_plus, dev_minus)
                self.copy(FW, c, *passed).start()
            else:
                self.copy(kind, c, *sends[kind]).start()

        def get(self, kind, c):
            self.copy(kind, c, gets[kind], dev_sib).wait_recv()

        def whole(self, kind, block):
            ref = self.view.at[:, rows(block)]
            return remote(ref, ss.at[self.which], rs.at[self.which, kind, 0], dev_sib)

        def share(self, kind):
            if self.shared:
                self.whole(kind, sends[kind][0]).start()

        def issue(self):
            for c, d in zip(LOW, HIGH):
                self.send(RP, c)
                self.send(RM, d)
            for c, d in zip(LOW, HIGH):
                self.send(RP, d)
                self.send(RM, c)
            self.share(B0)

        def issue_chunk(self, c):
            self.send(RP, c)
            self.send(RM, c)

        def step1(self):
            for c, d in zip(LOW, HIGH):
                self.get(RP, c)
                self.send(FW, c)
                self.get(RM, d)
                self.send(FW, d)

        def step2(self):
            for c in HIGH:
                self.get(RP, c)
            self.share(BM)
            for c in LOW:
                self.get(RM, c)
            self.share(BP)

        def step3(self):
            for c, d in zip(LOW, HIGH):
                for n in (c, d):
                    self.get(FW, n)
                    if self.shared:
                        ref = chunk(self.view, blk_across, n, CHUNKS)
                        remote(ref, ss.at[self.which], rs.at[self.which, BX, 0], dev_sib).start()

        def finish(self, *kinds):
            for kind in kinds:
                self.whole(kind, gets[kind]).wait_recv()

        def drain(self, blocks):
            ref = self.view.at[:, pl.ds(0, half * blocks)]
            remote(ref, ss.at[self.which], rs.at[self.which, RP, 0], dev_sib).wait_send()

    ring_rw, ring_s = Ring(rw, G_RW), Ring(sbuf, G_S)
    ring_r, ring_l = Ring(raw, G_R), Ring(lbuf, G_L, shared=False)
    chip_l = Ring(lbuf, G_L)

    def over_y(view, which, c, count, block=row):
        return remote(chunk(view, block, c, count), vs.at[which], vr.at[which, c], dev_y)

    l_blocks = (row, blk_minus, blk_plus, blk_across)

    def l_over_y(n, c):
        ref = chunk(lbuf, l_blocks[n], c, 4)
        return remote(ref, vs.at[Y_L], vr.at[Y_L + n, c], dev_y)

    def y_drain(view, which, blocks):
        ref = view.at[:, pl.ds(0, half * blocks)]
        remote(ref, vs.at[which], vr.at[which, 0], dev_y).wait_send()

    def ang_copy():
        return remote(ang.at[0], vs.at[Y_ANG], vr.at[Y_ANG, 0], dev_y)

    def load_sites(view):
        copies = [
            pltpu.make_async_copy(sites.at[0, :, s], view.at[s, own], loc.at[s]) for s in range(2)
        ]
        for copy in copies:
            copy.start()
        for copy in copies:
            copy.wait()

    for n in range(2):
        ang[parity, 8 * n : 8 * n + 8, :] = jnp.full((8, 128), angles[0, n], F32)

    def scalar(n):
        return trig[n, 0:1, 0:1]

    @pl.when(is_left)
    def _():
        load_sites(lbuf)

    @pl.when(is_right)
    def _():
        fetch = pltpu.make_async_copy(sketch, wbuf, loc.at[2])
        fetch.start()
        load_sites(raw)
        kick = ang[1, 0:8, :]
        trig[4] = jnp.cos(kick)
        trig[5] = jnp.sin(kick)
        cb, sb = scalar(4), scalar(5)
        r0, r1 = raw[0, own, :], raw[1, own, :]
        mixed = above(
            beside(cb * r0 - sb * r1, sb * r0 + cb * r1),
            beside(cb * r1 - sb * r0, cb * r0 + sb * r1),
        )
        fetch.wait()
        high, low = split(wbuf[...])
        wh[...] = high
        wl[...] = low
        result = dot3(split(mixed), (wh[...], wl[...]))
        for m in range(2):
            rw[m, own, :] = result[half * m : half * (m + 1)]

    @pl.when(is_left)
    def _():
        pl.semaphore_wait(barrier, 4)
        pl.semaphore_signal(ready, inc=1, device_id=dev_y, device_id_type=MESH)

    @pl.when(is_right)
    def _():
        pl.semaphore_wait(barrier, 3)

    def all_trig():
        ang_copy().wait_recv()
        kick, coupling = ang[0, 0:8, :], 0.5 * (ang[0, 8:16, :] + ang[1, 8:16, :])
        trig[0] = jnp.cos(kick)
        trig[1] = jnp.sin(kick)
        trig[2] = jnp.cos(coupling)
        trig[3] = jnp.sin(coupling)

    def rows_of_s():
        ca, sa, cj, sj = (scalar(n) for n in range(4))
        l0, l1 = lbuf[0, own, :], lbuf[1, own, :]
        p, q = ca * l0 - sa * l1, sa * l0 + ca * l1
        lhs = above(beside(cj * p, sj * q), beside(cj * q, -sj * p))
        result = dot3(split(lhs), split(rw[...].reshape(2 * width, width)))
        for s in range(2):
            sbuf[s, own, :] = result[half * s : half * (s + 1)]

    @pl.when(is_right)
    def _():
        ring_rw.issue()
        ring_rw.step1()
        ring_rw.step2()
        all_trig()
        for c in range(4):
            l_over_y(0, c).wait_recv()
        ring_rw.step3()
        ring_rw.finish(B0, BM, BP, BX)
        rows_of_s()
        pl.semaphore_wait(ready, 1)
        for c in (0, 2, 1, 3):
            over_y(sbuf, Y_S, c, 4).start()
        ring_s.issue()
        chip_l.share(B0)
        ring_s.step1()
        ring_r.issue()
        ring_s.step2()

    @pl.when(is_left)
    def _():
        ang_copy().start()
        for c in range(4):
            l_over_y(0, c).start()
        ring_l.issue()
        ring_l.step1()
        for c in range(2):
            l_over_y(1, c).start()
            l_over_y(2, c + 2).start()
        ring_l.step2()
        for c in range(2):
            l_over_y(1, c + 2).start()
            l_over_y(2, c).start()
        ring_l.step3()
        for c in range(4):
            l_over_y(3, c).start()
        for c in (0, 2, 1, 3):
            over_y(sbuf, Y_S, c, 4).wait_recv()
            ring_s.issue_chunk(c)
        ring_s.share(B0)
        ring_s.step1()
        ring_s.step2()

    cut = width // 2

    def add_gram(where, first=False):
        two = pl.ds(pl.multiple_of(2 * half * where, 2 * half), 2 * half)
        pair = split(above(sbuf[0, two, :], sbuf[1, two, :]))
        right = tuple(n[:, cut:] for n in pair)
        top = dot3(tuple(n[:, :cut] for n in pair), pair, ((0,), (0,)))
        low = dot3(right, right, ((0,), (0,)))
        if first:
            zf[:cut, :] = top
            zf[cut:, cut:] = low
        else:
            zf[:cut, :] += top
            zf[cut:, cut:] += low

    ring_s.finish(B0)
    add_gram(place, first=True)
    ring_s.finish(BM, BP)
    add_gram(minus)
    add_gram(plus)
    ring_s.step3()
    at_row = lax.broadcasted_iota(jnp.int32, (2 * half, width), 0)
    at_col = lax.broadcasted_iota(jnp.int32, (2 * half, width), 1)
    unit = jnp.where((at_col == at_row + half * row) & (at_row < half), 1.0, 0.0).astype(F32)
    mine = above(sbuf[0, own, :], sbuf[1, own, :])
    xbuf[...] = jnp.where(is_left, mine, unit)
    ring_s.finish(BX)
    add_gram(across)
    top, low = zf[:cut, :], zf[cut:, cut:]
    squares = jnp.sum(top * top) + jnp.sum(low * low) + jnp.sum(top[:, cut:] * top[:, cut:])
    scale = jnp.sqrt(jnp.full((1, 1), squares, F32) + 1e-06)
    per = 1.0 / scale
    zf[:cut, :] = top * per
    zf[cut:, :cut] = top[:, cut:].T * per
    zf[cut:, cut:] = low * per

    def refine():
        z, x = zf[...], xbuf[...]
        z2 = split(z)
        zr = tuple(n[:, cut:] for n in z2)
        top = dot3(tuple(n[:cut] for n in z2), z2)
        low = dot3(tuple(n[cut:] for n in z2), zr)
        top2, low2 = split(top), split(low)
        under = tuple(beside(a[:, cut:].T, b) for a, b in zip(top2, low2))
        new_top = 2.25 * z[:cut] - 1.5 * top + 0.25 * dot3(top2, z2)
        new_low = 2.25 * z[cut:, cut:] - 1.5 * low + 0.25 * dot3(under, zr)
        xbuf[...] = 1.5 * x - 0.5 * rows3(split(x), z2)
        zf[:cut, :] = new_top
        zf[cut:, :cut] = new_top[:, cut:].T
        zf[cut:, cut:] = new_low

    for _ in range((ITERS - 2) // 2):
        refine()

    @pl.when(is_right)
    def _():
        ring_r.step1()
        for n, kind in ((1, BM), (2, BP)):
            for c in range(4):
                l_over_y(n, c).wait_recv()
            chip_l.share(kind)

    for _ in range((ITERS - 2) // 2):
        refine()

    @pl.when(is_right)
    def _():
        ring_r.step2()
        for c in range(4):
            l_over_y(3, c).wait_recv()
        chip_l.share(BX)
        ring_r.step3()

    z2, x = split(zf[...]), xbuf[...]

    def times_z(rows_):
        return rows3(split(rows_), z2)

    moved = times_z(x)
    x = 1.5 * x - 0.5 * moved
    turned = 1.5 * moved - 0.5 * times_z(moved)
    for _ in range(2):
        turned = 1.5 * turned - 0.5 * times_z(turned)
    x = 1.5 * x - 0.5 * turned

    gain = jnp.sqrt(2.0 * width / scale)

    @pl.when(is_left)
    def _():
        obuf[...] = (x * gain).reshape(2, half, width)

    @pl.when(is_right)
    def _():
        chip_l.finish(B0, BM, BP, BX)
        ring_r.finish(B0, BM, BP, BX)
        ca, sa, cj, sj, cb, sb = (scalar(n) for n in range(6))
        cols = split(x[:half] * gain)
        e0, e1 = (
            rows3(cols, split(sbuf[s]), ((1,), (1,))) for s in range(2)
        )
        f, g = ca * e0 + sa * e1, ca * e1 - sa * e0
        lhs = above(beside(cj * f, cj * g), beside(-sj * g, sj * f))
        both = rows3(split(lhs), split(lbuf[...].reshape(2 * width, width)))
        c0, c1 = both[:half], both[half:]
        lhs = above(
            beside(cb * c0 - sb * c1, cb * c1 - sb * c0),
            beside(sb * c0 + cb * c1, cb * c0 + sb * c1),
        )
        right = rows3(split(lhs), split(raw[...].reshape(2 * width, width)))
        obuf[...] = (right * (1.0 / (2.0 * width))).reshape(2, half, width)

    stores = [
        pltpu.make_async_copy(obuf.at[s], out.at[0, :, s], loc.at[s]) for s in range(2)
    ]
    for store in stores:
        store.start()

    ring_s.drain(7)

    @pl.when(is_left)
    def _():
        ang_copy().wait_send()
        y_drain(lbuf, Y_L, 4)
        ring_l.drain(3)

    @pl.when(is_right)
    def _():
        y_drain(sbuf, Y_S, 1)
        ring_rw.drain(7)
        ring_r.drain(7)
        chip_l.drain(4)

    for store in stores:
        store.wait()


def per_device(sites, angles, sketch):
    half, width = sites.shape[1], sites.shape[3]
    dma, vmem = pltpu.SemaphoreType.DMA, pltpu.VMEM
    return pl.pallas_call(
        kernel,
        out_shape=jax.ShapeDtypeStruct(sites.shape, F32),
        in_specs=[
            pl.BlockSpec(memory_space=pl.ANY),
            pl.BlockSpec(memory_space=pltpu.SMEM),
            pl.BlockSpec(memory_space=pl.ANY),
        ],
        out_specs=pl.BlockSpec(memory_space=pl.ANY),
        scratch_shapes=[
            vmem((2, width, width), F32),
            vmem((2, width, width), F32),
            vmem((2, width, width), F32),
            vmem((2, width, width), F32),
            vmem((2 * width, width), F32),
            vmem((2 * width, width), BF16),
            vmem((2 * width, width), BF16),
            vmem((width, width), F32),
            vmem((2 * half, width), F32),
            vmem((2, half, width), F32),
            vmem((2, 16, 128), F32),
            vmem((6, 8, 128), F32),
            dma((4,)), dma((4, 7, 4)),
            dma((6,)), dma((6, 4)),
            dma((3,)), pltpu.SemaphoreType.REGULAR,
        ],
        compiler_params=pltpu.CompilerParams(
            collective_id=0, has_side_effects=True, vmem_limit_bytes=56 * 2**20
        ),
        cost_estimate=pl.CostEstimate(
            flops=20 * 6 * width**3, bytes_accessed=3 * 2**20, transcendentals=0
        ),
    )(sites, angles, sketch)


def solution(mesh):
    in_specs = (P("chain", "rows", None, None), P("chain", None), P())
    out_specs = P("chain", "rows", None, None)
    return jax.shard_map(
        per_device, mesh=mesh, in_specs=in_specs, out_specs=out_specs, check_vma=False
    )
```
